128 devices in a mesh: batch: 8 (over z, core), table: 16 (over y, x).
Axes of the slice: x: 4, y: 4, z: 4, core: 2. Of those that a mesh axis runs over, the one named last changes fastest.
Arguments:
- item_rows: int32 [1024, 64, 3], P(('batch', 'table')), may hold values from 0 to 16383, as said below
- send_order: int32 [1024], P(('batch', 'table')), may hold values from 0 to 7, as said below
- user_lengths: int32 [1024], P(('batch', 'table')), may hold values from 1 to 64, as said below
- tables: bfloat16 [3, 16384, 1024], P(None, 'table'), may hold values from -3 to 3
- w_in: bfloat16 [1, 1024, 4096], replicated, may hold values from -0.1875 to 0.1875
- w_out: bfloat16 [1, 1024, 1024], replicated, may hold values from -0.1875 to 0.1875
- out_grad: bfloat16 [1024, 64, 1024], P(('batch', 'table')), may hold values from -6 to 6
Outputs:
- encoded: bfloat16 [1024, 64, 1024], P(('batch', 'table'))
- table_grad: float32 [3, 16384, 1024], P(None, 'table', 'batch')
The draws below stay inside these ranges and needn't reach their ends.
Inputs may be any that keep to these rules, and one draw needn't show every extreme that they name: `item_rows`: every id lies in one table's rows. For each user, the 192 ids name rows of each block of 1024 rows exactly 12 times; padded slots carry ids too. `send_order`: each block of 8 entries is a permutation of 0 to 7. `user_lengths`: the first user of every block of 8 has length 64.
All inputs are finite; a program needn't handle non-finite values.
Results may differ from the reference program's by a relative error of at most 0.013.
Values may be sent and summed in bfloat16 or wider, within the bound.
No kernel may reach another device: no remote copies, remote signals or barrier semaphores. Data moves between devices by JAX's collectives and lax.ppermute only.
A program may use at most 192 MiB of HBM per device.

```python
import jax
import jax.numpy as jnp
from jax import lax

D = 1024
HEADS = 8
LAYERS = 1
LEN = 64
USER_DEV = 8
ROWS_DEV = 1024
HIDDEN_SIZE = 4096
SHARDS = 16
ROWS = 16384
USERS = 1024
N_BATCH = 8
N_TABLE = 16


def draw_item_rows(key, part):
    key = jax.random.fold_in(key, 11)
    entry_count = 3 * LEN
    order_keys = jax.random.split(jax.random.fold_in(key, 1), USERS)
    orders = jax.vmap(lambda one_key: jax.random.permutation(one_key, entry_count))(order_keys)
    owner_rank = orders % SHARDS
    first = jax.random.randint(jax.random.fold_in(key, 2), (USERS, entry_count), 0, ROWS_DEV)
    second = jax.random.randint(jax.random.fold_in(key, 3), (USERS, entry_count), 0, ROWS_DEV)
    local_row = first * second // ROWS_DEV
    return (owner_rank * ROWS_DEV + local_row).astype(jnp.int32).reshape(USERS, LEN, 3)


def draw_send_order(key, part):
    key = jax.random.fold_in(key, 12)
    device_keys = jax.random.split(key, USERS // USER_DEV)
    orders = jax.vmap(lambda one_key: jax.random.permutation(one_key, USER_DEV))(device_keys)
    return orders.reshape(USERS).astype(jnp.int32)


def draw_user_lengths(key, part):
    key = jax.random.fold_in(key, 13)
    first = jax.random.randint(jax.random.fold_in(key, 1), (USERS,), 1, LEN + 1)
    second = jax.random.randint(jax.random.fold_in(key, 2), (USERS,), 1, LEN + 1)
    lengths = jnp.maximum(first * second // LEN, 1)
    heavy = jnp.arange(USERS) % USER_DEV == 0
    return jnp.where(heavy, LEN, lengths).astype(jnp.int32)


def levels(key, shape, pieces, low, high):
    gain = 1.0
    for position, shards_of in pieces:
        heights = jax.random.uniform(jax.random.fold_in(jax.random.fold_in(key, 6), position), (shards_of,), jnp.float32, low / len(pieces), high / len(pieces))
        gain = gain * jnp.repeat(jnp.exp(heights), shape[position] // shards_of).reshape((-1,) + (1,) * (len(shape) - 1 - position))
    return gain


def gaussian(own_key, dims, spread, bound, shards=(), kind=jnp.bfloat16):
    loudness = levels(own_key, dims, shards, -0.22, 0.18) if shards else 1.0
    values = jax.random.normal(own_key, dims, jnp.float32) * spread * loudness
    return jnp.minimum(jnp.maximum(values, -bound), bound).astype(kind)


def setup_inputs(seed: int = 0) -> dict:
    arg_keys = jax.random.split(jax.random.key(seed), 8)
    return {
        "item_rows": draw_item_rows(jax.random.fold_in(arg_keys[7], 71), 0),
        "send_order": draw_send_order(jax.random.fold_in(arg_keys[7], 71), 0),
        "user_lengths": draw_user_lengths(jax.random.fold_in(arg_keys[7], 71), 0),
        "tables": gaussian(arg_keys[3], (3, ROWS, D), 0.5, 3.0, ((1, 16),)),
        "w_in": gaussian(arg_keys[4], (LAYERS, D, HIDDEN_SIZE), D ** -0.5, 0.1875),
        "w_out": gaussian(arg_keys[5], (LAYERS, D, D), D ** -0.5, 0.1875),
        "out_grad": gaussian(arg_keys[6], (USERS, LEN, D), 1.0, 6.0, ((0, 128),)),
    }


epsilon = 1e-05

def normalize_rows(stream):
    center_mean = lax.optimization_barrier(jnp.mean(stream, axis=-1, keepdims=True))
    centered = stream - center_mean
    variance = lax.optimization_barrier(jnp.mean(centered * centered, axis=-1, keepdims=True))
    return centered * lax.rsqrt(variance + epsilon)

def hstu_block(stream, w_in_layer, w_out_layer, attend_mask):
    user_count, seq_length, model_width = stream.shape
    head_size = model_width // HEADS
    normed = normalize_rows(stream).astype(jnp.bfloat16).reshape(user_count * seq_length, model_width)
    projected = jax.nn.silu(jnp.dot(normed, w_in_layer, preferred_element_type=jnp.float32))
    projected = projected.reshape(user_count, seq_length, 4, model_width)
    gate_part = projected[:, :, 0]
    value_part = projected[:, :, 1].astype(jnp.bfloat16).reshape(user_count, seq_length, HEADS, head_size)
    query_part = projected[:, :, 2].astype(jnp.bfloat16).reshape(user_count, seq_length, HEADS, head_size)
    key_part = projected[:, :, 3].astype(jnp.bfloat16).reshape(user_count, seq_length, HEADS, head_size)
    scores = jnp.einsum('uqhe,ukhe->uhqk', query_part.astype(jnp.float32), key_part.astype(jnp.float32))
    scores = scores * head_size ** (-0.5)
    weights = (jax.nn.silu(scores) * attend_mask).astype(jnp.bfloat16)
    mixed = jnp.einsum('uhqk,ukhe->uqhe', weights.astype(jnp.float32), value_part.astype(jnp.float32))
    mixed = mixed.reshape(user_count, seq_length, model_width)
    gated = (normalize_rows(mixed) * gate_part).astype(jnp.bfloat16).reshape(user_count * seq_length, model_width)
    update = jnp.dot(gated, w_out_layer, preferred_element_type=jnp.float32)
    return stream + update.reshape(user_count, seq_length, model_width)

def stack_forward(stream, w_in, w_out, attend_mask, live_slots):
    for layer_index in range(LAYERS):
        if layer_index > 0:
            stream = lax.optimization_barrier(stream.astype(jnp.bfloat16)).astype(jnp.float32)
        stream = hstu_block(stream, w_in[layer_index], w_out[layer_index], attend_mask)
    return stream * live_slots[:, :, None]

def run_layers(embedded, lengths, cotangent, w_in, w_out):
    seq_length = embedded.shape[1]
    positions = jnp.arange(seq_length, dtype=jnp.int32)
    live_bool = positions[None, :] < lengths[:, None]
    live_slots = live_bool.astype(jnp.float32)
    causal = positions[None, :] <= positions[:, None]
    attend_mask = (causal[None, None, :, :] & live_bool[:, None, :, None]).astype(jnp.float32)

    def forward(stream):
        return stack_forward(stream, w_in, w_out, attend_mask, live_slots)
    output, pullback = jax.vjp(forward, embedded.astype(jnp.float32))
    token_grad = pullback(cotangent.astype(jnp.float32))[0]
    return (output.astype(jnp.bfloat16), token_grad)

def device_block(moved_ids, lengths, cotangent, tables, w_in, w_out):
    total = tables[0][moved_ids[:, :, 0]].astype(jnp.float32)
    total = total + tables[1][moved_ids[:, :, 1]].astype(jnp.float32)
    total = total + tables[2][moved_ids[:, :, 2]].astype(jnp.float32)
    embedded = total.astype(jnp.bfloat16)
    return run_layers(embedded, lengths, cotangent, w_in, w_out)

def reference(item_rows, send_order, user_lengths, tables, w_in, w_out, out_grad):
    device_count = N_BATCH * N_TABLE
    per_rank = USER_DEV // N_BATCH
    slot_index = jnp.arange(USERS, dtype=jnp.int32)
    device_index = slot_index // USER_DEV
    local_slot = slot_index % USER_DEV
    batch_rank = device_index // N_TABLE
    table_rank = device_index % N_TABLE
    source_rank = local_slot // per_rank
    within_rank = local_slot % per_rank
    source_device = source_rank * N_TABLE + table_rank
    picked_user = send_order[source_device * USER_DEV + batch_rank * per_rank + within_rank]
    moved_ids = item_rows[(source_device * USER_DEV + picked_user).astype(jnp.int32)]
    id_blocks = moved_ids.reshape(device_count, USER_DEV, LEN, 3)
    length_blocks = user_lengths.reshape(device_count, USER_DEV)
    grad_blocks = out_grad.reshape(device_count, USER_DEV, LEN, D)

    def one_device(item):
        return device_block(item[0], item[1], item[2], tables, w_in, w_out)
    encoded, token_grad = lax.map(one_device, (id_blocks, length_blocks, grad_blocks))
    token_grad = token_grad.reshape(USERS * LEN, D)
    flat_ids = moved_ids.reshape(USERS * LEN, 3)
    table_grad = jnp.stack([jnp.zeros((ROWS, D), jnp.float32).at[flat_ids[:, hash_index]].add(token_grad) for hash_index in range(3)])
    return (encoded.reshape(USERS, LEN, D), table_grad)
```

```python
import functools

import jax
import jax.numpy as jnp
from jax import lax
from jax.experimental import pallas as pl
from jax.experimental.pallas import tpu as pltpu
from jax.sharding import PartitionSpec as P

HEADS = 8
PER = 12
EPS = 1e-05
BF = jnp.bfloat16
F32 = jnp.float32
NT = (((1,), (1,)), ((), ()))
NN = (((1,), (0,)), ((), ()))
TN = (((0,), (0,)), ((), ()))
CHUNKS = 2
VMEM_LIMIT = 48 * 1024 * 1024


def dot(a, b, dims=NN):
    return lax.dot_general(a, b, dims, preferred_element_type=F32)


def iota(shape, dim):
    return lax.broadcasted_iota(jnp.int32, shape, dim)


def ids_kernel(order_ref, ids_ref, out_ref, ids_scr):
    users, owners = out_ref.shape[0], out_ref.shape[1]
    hashes, _, length = ids_ref.shape
    ids_scr[...] = jnp.full(ids_scr.shape, -1, jnp.int32)
    for b in range(users):
        user = order_ref[b]
        for h in range(hashes):
            ids_scr[b : b + 1, h * length : (h + 1) * length] = ids_ref[h, pl.ds(user, 1), :]
    ids = ids_scr[...]
    lanes = ids.shape[1]
    owner = lax.shift_right_arithmetic(ids, 10)
    hash_of = lax.div(iota(ids.shape, 1), length)
    code = (ids & 1023) + 1024 * hash_of
    high = (lax.shift_right_logical(code, 6)).astype(F32)
    low = (code & 63).astype(F32)
    hits = [jnp.where(owner == o, 1.0, 0.0).astype(F32) for o in range(owners)]
    before = jnp.where(iota((lanes, lanes), 0) < iota((lanes, lanes), 1), 1.0, 0.0).astype(BF)
    prefix = dot(jnp.concatenate(hits, axis=0).astype(BF), before)
    rank = jnp.zeros(ids.shape, F32)
    for o in range(owners):
        rank = rank + hits[o] * prefix[o * users : (o + 1) * users]
    rank = rank.astype(jnp.int32)
    total = jnp.zeros((2 * owners, 128), F32)
    for b in range(users):
        hit = iota((owners, lanes), 0) == owner[b : b + 1]
        left = jnp.concatenate(
            [jnp.where(hit, high[b : b + 1], 0.0), jnp.where(hit, low[b : b + 1], 0.0)], axis=0
        ).astype(BF)
        right = jnp.where(iota((128, lanes), 0) == rank[b : b + 1] + PER * b, 1.0, 0.0).astype(BF)
        total = total + dot(left, right, NT)
    codes = (total[:owners] * 64.0 + total[owners:]).astype(jnp.int32)
    slots = owner * 16 + rank
    for b in range(users):
        out_ref[b, :, :128] = codes
        out_ref[b, :, 128:] = jnp.broadcast_to(slots[b : b + 1], (owners, lanes))


def leaving_ids(order, ids, owners):
    users = ids.shape[1]
    return pl.pallas_call(
        ids_kernel,
        out_shape=jax.ShapeDtypeStruct((users, owners, 384), jnp.int32),
        in_specs=[
            pl.BlockSpec(memory_space=pltpu.SMEM),
            pl.BlockSpec(memory_space=pltpu.VMEM),
        ],
        out_specs=pl.BlockSpec(memory_space=pltpu.VMEM),
        scratch_shapes=[pltpu.VMEM((users, 256), jnp.int32)],
        compiler_params=pltpu.CompilerParams(vmem_limit_bytes=VMEM_LIMIT),
        name="leaving_ids",
    )(order, ids)


def serve_kernel(rank_ref, code_ref, table_hbm, *refs):
    outs = refs[:CHUNKS]
    raw, wide, stage, sems = refs[CHUNKS:]
    hashes, rows, width = table_hbm.shape
    tiles = width // 128
    copies = [
        pltpu.make_async_copy(table_hbm.at[h], raw.at[h], sems.at[h]) for h in range(hashes)
    ]
    for copy in copies:
        copy.start()
    for h in range(hashes):
        copies[h].wait()

        @pl.loop(0, rows // 16)
        def _(g):
            first = pl.multiple_of(g * 16, 16)
            for c in range(tiles):
                both = raw[h, pl.ds(first, 16), c * 128 : (c + 1) * 128].astype(F32)
                base = (h * rows + first) * tiles + c
                wide[pl.ds(base, 8, stride=tiles), :] = both[:8]
                wide[pl.ds(base + 8 * tiles, 8, stride=tiles), :] = both[8:]

    first_lane = rank_ref[0] * PER
    requesters, per_chunk, _ = outs[0].shape
    chunk_users = per_chunk // PER
    for chunk in range(CHUNKS):
        out_ref = outs[chunk]

        @pl.loop(0, requesters)
        def _(t):
            for j in range(chunk_users):
                home = (chunk * chunk_users + j) * requesters + t
                for k in range(PER):
                    row = code_ref[home, first_lane + k]
                    slot = (j * PER + k) * tiles
                    stage[slot : slot + tiles, :] = wide[
                        pl.ds(pl.multiple_of(row * tiles, tiles), tiles), :
                    ]
            for g in range(per_chunk // 16):
                for c in range(tiles):
                    base = g * 16 * tiles + c
                    upper = stage[pl.ds(base, 8, stride=tiles), :]
                    lower = stage[pl.ds(base + 8 * tiles, 8, stride=tiles), :]
                    out_ref[t, g * 16 : (g + 1) * 16, c * 128 : (c + 1) * 128] = jnp.concatenate(
                        [upper, lower], axis=0
                    ).astype(BF)


def serve_rows(rank, got, tables, requesters, per_chunk):
    hashes, rows, width = tables.shape
    tiles = width // 128
    return pl.pallas_call(
        serve_kernel,
        out_shape=[jax.ShapeDtypeStruct((requesters, per_chunk, width), BF)] * CHUNKS,
        grid=(1,),
        in_specs=[
            pl.BlockSpec(memory_space=pltpu.SMEM),
            pl.BlockSpec((got.shape[0], 128), lambda i: (0, 0), memory_space=pltpu.SMEM),
            pl.BlockSpec(memory_space=pl.ANY),
        ],
        out_specs=[pl.BlockSpec((requesters, per_chunk, width), lambda i: (0, 0, 0))] * CHUNKS,
        scratch_shapes=[
            pltpu.VMEM((hashes, rows, width), BF),
            pltpu.VMEM((hashes * rows * tiles, 128), F32),
            pltpu.VMEM((per_chunk * tiles, 128), F32),
            pltpu.SemaphoreType.DMA((hashes,)),
        ],
        compiler_params=pltpu.CompilerParams(vmem_limit_bytes=VMEM_LIMIT),
        name="serve_rows",
    )(rank, got, tables)


def sigmoid(z):
    return 0.5 + 0.5 * jnp.tanh(0.5 * z)


def layer_kernel(
    chunk, len_ref, slot_ref, fetched_ref, cot_ref, w_in_hbm, w_out_hbm, enc_ref, grad_ref,
    win, wout, x_s, n_s, gate_s, dsilu_s, qkv_s, mixed_s, w_s, dw_s, dz_s, live_s, sems,
):
    users, length, width = cot_ref.shape
    tokens = users * length
    head = width // HEADS
    owners, per_chunk, _ = fetched_ref.shape
    slots = owners * per_chunk
    pair = 2 * length
    pairs = tokens // pair
    copies = [
        pltpu.make_async_copy(
            w_in_hbm.at[0, :, pl.ds(c * width, width)], win.at[c], sems.at[c]
        )
        for c in range(4)
    ] + [pltpu.make_async_copy(w_out_hbm.at[0], wout, sems.at[4])]
    for copy in copies:
        copy.start()

    slot_rows = []
    for h in range(3):
        packed = slot_ref[h : h + 1, :]
        slot_rows.append(
            lax.shift_right_logical(packed, 4) * per_chunk
            + lax.div(iota((1, tokens), 1), length) * PER
            + (packed & 15)
        )
    stacked = jnp.concatenate(slot_rows + [jnp.zeros((5, tokens), jnp.int32)], axis=0)
    slot_cols = stacked.astype(F32).T.astype(jnp.int32)
    lane = iota((tokens, slots), 1)
    pick = (
        (lane == slot_cols[:, 0:1]) | (lane == slot_cols[:, 1:2]) | (lane == slot_cols[:, 2:3])
    )
    pick = jnp.where(pick, 1.0, 0.0).astype(BF)
    x = dot(pick, fetched_ref[...].reshape(slots, width)).astype(BF).astype(F32)
    x_s[...] = x
    mean = jnp.mean(x, axis=1, keepdims=True)
    centered = x - mean
    rstd = lax.rsqrt(jnp.mean(centered * centered, axis=1, keepdims=True) + EPS)
    n_s[...] = (centered * rstd).astype(BF)

    token_user = lax.div(iota((tokens, 1), 0), length)
    token_pos = iota((tokens, 1), 0) - token_user * length
    token_len = jnp.zeros((tokens, 1), jnp.int32)
    for u in range(users):
        token_len = jnp.where(token_user == u, len_ref[chunk * users + u], token_len)
    live = jnp.where(token_pos < token_len, 1.0, 0.0).astype(F32)
    key = iota((tokens, pair), 1)
    query = iota((tokens, pair), 0)
    same = lax.div(key, length) == lax.rem(lax.div(query, length), 2)
    causal = lax.rem(key, length) <= lax.rem(query, length)
    live_s[...] = jnp.where(same & causal, 1.0, 0.0) * live

    step = 256
    for c in range(4):
        copies[c].wait()

        @pl.loop(0, width // step)
        def _(i):
            cols = pl.ds(pl.multiple_of(i * step, step), step)
            z = dot(n_s[...], win[c, :, cols])
            sig = sigmoid(z)
            out = z * sig
            dsilu_s[c, :, cols] = sig + out * (1.0 - sig)
            if c == 0:
                gate_s[:, cols] = out
            else:
                qkv_s[c - 1, :, cols] = out.astype(BF)

    scale = head ** (-0.5)
    for p in range(pairs):
        rows = slice(p * pair, (p + 1) * pair)
        for h in range(HEADS):
            cols = slice(h * head, (h + 1) * head)
            s = dot(qkv_s[1, rows, cols], qkv_s[2, rows, cols], NT) * scale
            mask = live_s[rows, :]
            sig = sigmoid(s)
            out = s * sig
            w = (out * mask).astype(BF)
            w_s[p * HEADS + h] = w
            dw_s[p * HEADS + h] = (sig + out * (1.0 - sig)) * (mask * scale)
            mixed_s[rows, cols] = dot(w, qkv_s[0, rows, cols])

    mixed = mixed_s[...]
    mean2 = jnp.mean(mixed, axis=1, keepdims=True)
    centered2 = mixed - mean2
    rstd2 = lax.rsqrt(jnp.mean(centered2 * centered2, axis=1, keepdims=True) + EPS)
    hat = centered2 * rstd2
    gate = gate_s[...]
    gated = (hat * gate).astype(BF)
    copies[4].wait()
    out = (x_s[...] + dot(gated, wout[...])) * live
    enc_ref[...] = out.astype(BF).reshape(users, length, width)

    g = cot_ref[...].reshape(tokens, width).astype(F32) * live
    dgated = dot(g.astype(BF), wout[...], NT).astype(BF).astype(F32)
    dz_s[0] = (dgated * hat * dsilu_s[0]).astype(BF)
    dhat = dgated * gate
    dmixed = rstd2 * (
        dhat
        - jnp.mean(dhat, axis=1, keepdims=True)
        - hat * jnp.mean(dhat * hat, axis=1, keepdims=True)
    )
    n_mixed = dmixed.astype(BF)
    for p in range(pairs):
        rows = slice(p * pair, (p + 1) * pair)
        for h in range(HEADS):
            cols = slice(h * head, (h + 1) * head)
            dm = n_mixed[rows, cols]
            v, q, k = (qkv_s[i, rows, cols] for i in range(3))
            dweights = dot(dm, v, NT).astype(BF).astype(F32)
            ds = (dweights * dw_s[p * HEADS + h]).astype(BF)
            dv = dot(w_s[p * HEADS + h], dm, TN).astype(BF).astype(F32)
            dq = dot(ds, k).astype(BF).astype(F32)
            dk = dot(ds, q, TN).astype(BF).astype(F32)
            dz_s[1, rows, cols] = (dv * dsilu_s[1, rows, cols]).astype(BF)
            dz_s[2, rows, cols] = (dq * dsilu_s[2, rows, cols]).astype(BF)
            dz_s[3, rows, cols] = (dk * dsilu_s[3, rows, cols]).astype(BF)

    @pl.loop(0, width // step)
    def _(i):
        cols = pl.ds(pl.multiple_of(i * step, step), step)
        dn = dot(dz_s[0], win[0, cols, :], NT)
        for c in range(1, 4):
            dn = dn + dot(dz_s[c], win[c, cols, :], NT)
        mixed_s[:, cols] = dn

    dn = mixed_s[...].astype(BF).astype(F32)
    x = x_s[...]
    xhat = (x - mean) * rstd
    dx = rstd * (
        dn
        - jnp.mean(dn, axis=1, keepdims=True)
        - xhat * jnp.mean(dn * xhat, axis=1, keepdims=True)
    )
    token_grad = (dx + g).astype(BF)
    n_s[...] = token_grad
    for t in range(owners):
        sub = iota((per_chunk, tokens), 0) + t * per_chunk
        put = (sub == slot_rows[0]) | (sub == slot_rows[1]) | (sub == slot_rows[2])
        rows_out = dot(jnp.where(put, 1.0, 0.0).astype(BF), n_s[...]).astype(BF)
        for b in range(grad_ref.shape[0]):
            grad_ref[b, t] = rows_out[:, b * 128 : (b + 1) * 128]


def layer(chunk, lengths, slots, fetched, cot, w_in, w_out, batch_ranks):
    owners, per_chunk, width = fetched.shape
    users, length, _ = cot.shape
    users //= CHUNKS
    tokens = users * length
    blocks = (users // 2) * HEADS
    return pl.pallas_call(
        functools.partial(layer_kernel, chunk),
        out_shape=[
            jax.ShapeDtypeStruct((users, length, width), BF),
            jax.ShapeDtypeStruct((batch_ranks, owners, per_chunk, width // batch_ranks), BF),
        ],
        grid=(1,),
        in_specs=[
            pl.BlockSpec(memory_space=pltpu.SMEM),
            pl.BlockSpec((3, tokens), lambda i: (0, 0)),
            pl.BlockSpec((owners, per_chunk, width), lambda i: (0, 0, 0)),
            pl.BlockSpec((users, length, width), lambda i: (chunk, 0, 0)),
            pl.BlockSpec(memory_space=pl.ANY),
            pl.BlockSpec(memory_space=pl.ANY),
        ],
        out_specs=[
            pl.BlockSpec((users, length, width), lambda i: (0, 0, 0)),
            pl.BlockSpec(
                (batch_ranks, owners, per_chunk, width // batch_ranks), lambda i: (0, 0, 0, 0)
            ),
        ],
        scratch_shapes=[
            pltpu.VMEM((4, width, width), BF),
            pltpu.VMEM((width, width), BF),
            pltpu.VMEM((tokens, width), F32),
            pltpu.VMEM((tokens, width), BF),
            pltpu.VMEM((tokens, width), F32),
            pltpu.VMEM((4, tokens, width), F32),
            pltpu.VMEM((3, tokens, width), BF),
            pltpu.VMEM((tokens, width), F32),
            pltpu.VMEM((blocks, 2 * length, 2 * length), BF),
            pltpu.VMEM((blocks, 2 * length, 2 * length), F32),
            pltpu.VMEM((4, tokens, width), BF),
            pltpu.VMEM((tokens, 2 * length), F32),
            pltpu.SemaphoreType.DMA((5,)),
        ],
        compiler_params=pltpu.CompilerParams(vmem_limit_bytes=VMEM_LIMIT),
        cost_estimate=pl.CostEstimate(
            flops=12_000_000_000 // CHUNKS, bytes_accessed=16_000_000, transcendentals=2_000_000
        ),
        name="layer",
    )(lengths, slots, fetched, cot, w_in, w_out)


def collect_kernel(first, *refs):
    if first:
        code_ref, rows_ref, out_ref = refs
    else:
        code_ref, rows_ref, prev_ref, out_ref = refs
    steps, depth = code_ref.shape
    tile = 512

    @pl.loop(0, out_ref.shape[0] // tile)
    def _(m):
        start = pl.multiple_of(m * tile, tile)
        acc = jnp.zeros((tile, 128), F32) if first else prev_ref[pl.ds(start, tile), :]
        for s in range(steps):
            hit = iota((tile, depth), 0) == code_ref[s : s + 1, :] - start
            acc = acc + dot(
                jnp.where(hit, 1.0, 0.0).astype(BF), rows_ref[s * depth : (s + 1) * depth, :]
            )
        out_ref[pl.ds(start, tile), :] = acc


def collect(codes, rows, prev, total):
    first = prev is None
    args = (codes, rows) if first else (codes, rows, prev)
    return pl.pallas_call(
        functools.partial(collect_kernel, first),
        out_shape=jax.ShapeDtypeStruct((total, 128), F32),
        in_specs=[pl.BlockSpec(memory_space=pltpu.VMEM)] * len(args),
        out_specs=pl.BlockSpec(memory_space=pltpu.VMEM),
        compiler_params=pltpu.CompilerParams(vmem_limit_bytes=VMEM_LIMIT),
        cost_estimate=pl.CostEstimate(
            flops=10_000_000_000 // CHUNKS, bytes_accessed=6_000_000, transcendentals=0
        ),
        name="collect",
    )(*args)


def body(item_rows, send_order, user_lengths, tables, w_in, w_out, out_grad):
    batch_ranks = lax.axis_size("batch")
    table_ranks = lax.axis_size("table")
    users, length, hashes = item_rows.shape
    rows_local = tables.shape[1]
    both = ("batch", "table")
    chunk_users = users // CHUNKS
    per_chunk = chunk_users * PER

    leaving = leaving_ids(send_order, item_rows.transpose(2, 0, 1), table_ranks)
    got = lax.all_to_all(
        leaving.reshape(batch_ranks * table_ranks, 384), both, 0, 0, tiled=True
    )
    homes = got.reshape(users, table_ranks, 384)
    rank = lax.axis_index("batch").astype(jnp.int32)[None]
    served = serve_rows(rank, got, tables, table_ranks, per_chunk)

    mine = lax.dynamic_index_in_dim(homes, lax.axis_index("table"), 1, keepdims=False)
    slots = mine[:, 128 : 128 + hashes * length].reshape(users, hashes, length)
    slots = slots.transpose(1, 0, 2)
    codes = homes[:, :, : batch_ranks * PER].reshape(users, table_ranks, batch_ranks, PER)
    codes = codes.transpose(2, 1, 0, 3)

    encoded, total = [], None
    returned = []
    for c in range(CHUNKS):
        part = slice(c * chunk_users, (c + 1) * chunk_users)
        fetched = lax.all_to_all(served[c], "table", 0, 0, tiled=True)
        enc, grads = layer(
            c, user_lengths, slots[:, part].reshape(hashes, chunk_users * length), fetched,
            out_grad, w_in, w_out, batch_ranks,
        )
        encoded.append(enc)
        grads = grads.reshape(batch_ranks * table_ranks, per_chunk, -1)
        returned.append(lax.all_to_all(grads, both, 0, 0, tiled=True))
    for c in range(CHUNKS):
        part = slice(c * chunk_users, (c + 1) * chunk_users)
        rows = returned[c].reshape(batch_ranks * table_ranks * per_chunk, -1)
        total = collect(
            codes[:, :, part].reshape(-1, 512), rows, total, hashes * rows_local
        )
    return jnp.concatenate(encoded, axis=0), total.reshape(hashes, rows_local, -1)


def solution(mesh):
    in_specs = (
        P(("batch", "table"), None, None),
        P(("batch", "table")),
        P(("batch", "table")),
        P(None, "table", None),
        P(),
        P(),
        P(("batch", "table"), None, None),
    )
    out_specs = (P(("batch", "table"), None, None), P(None, "table", "batch"))
    return jax.shard_map(body, mesh=mesh, in_specs=in_specs, out_specs=out_specs, check_vma=False)
```

```python
import functools

import jax
import jax.numpy as jnp
from jax import lax
from jax.experimental import pallas as pl
from jax.experimental.pallas import tpu as pltpu
from jax.sharding import PartitionSpec as P

HEADS = 8
PER = 12
EPS = 1e-05
BF = jnp.bfloat16
F32 = jnp.float32
NT = (((1,), (1,)), ((), ()))
NN = (((1,), (0,)), ((), ()))
TN = (((0,), (0,)), ((), ()))
CHUNKS = 2
MIB = 1024 * 1024
LAYER_VMEM = 49 * MIB
COLLECT_VMEM = 52 * MIB
PARTS = 4
OWNERS = 16
GROUP = 16
COST = pl.CostEstimate(flops=12_000_000_000, bytes_accessed=20_000_000, transcendentals=0)
PARTS_ORDER = (2, 3, 1, 0)
STEP = 256


def dot(a, b, dims=NN):
    return lax.dot_general(a, b, dims, preferred_element_type=F32)


def iota(shape, dim):
    return lax.broadcasted_iota(jnp.int32, shape, dim)


def ids_kernel(order_hbm, ids_hbm, out_hbm, order, raw, ids_scr, out, sems):
    hashes, users, length = raw.shape
    owners = out.shape[0] // users
    get_order = pltpu.make_async_copy(order_hbm, order, sems.at[0])
    get_ids = pltpu.make_async_copy(ids_hbm, raw, sems.at[1])
    get_order.start()
    get_ids.start()
    ids_scr[...] = jnp.full(ids_scr.shape, -1, jnp.int32)
    get_order.wait()
    get_ids.wait()
    for b in range(users):
        user = order[b]
        for h in range(hashes):
            ids_scr[b : b + 1, h * length : (h + 1) * length] = raw[h, pl.ds(user, 1), :]
    ids = ids_scr[...]
    lanes = ids.shape[1]
    owner = lax.shift_right_arithmetic(ids, 10)
    hash_of = lax.div(iota(ids.shape, 1), length)
    code = (ids & 1023) + 1024 * hash_of
    high = (lax.shift_right_logical(code, 6)).astype(F32)
    low = (code & 63).astype(F32)
    hits = [jnp.where(owner == o, 1.0, 0.0).astype(F32) for o in range(owners)]
    before = jnp.where(iota((lanes, lanes), 0) < iota((lanes, lanes), 1), 1.0, 0.0).astype(BF)
    prefix = dot(jnp.concatenate(hits, axis=0).astype(BF), before)
    rank = jnp.zeros(ids.shape, F32)
    for o in range(owners):
        rank = rank + hits[o] * prefix[o * users : (o + 1) * users]
    rank = rank.astype(jnp.int32)
    total = jnp.zeros((2 * owners, 128), F32)
    for b in range(users):
        hit = iota((owners, lanes), 0) == owner[b : b + 1]
        left = jnp.concatenate(
            [jnp.where(hit, high[b : b + 1], 0.0), jnp.where(hit, low[b : b + 1], 0.0)], axis=0
        ).astype(BF)
        right = jnp.where(iota((128, lanes), 0) == rank[b : b + 1] + PER * b, 1.0, 0.0).astype(BF)
        total = total + dot(left, right, NT)
    codes = (total[:owners] * 64.0 + total[owners:]).astype(jnp.int32)
    slots = owner * 16 + rank
    for b in range(users):
        part = pl.ds(b * owners, owners)
        out[part, 0, :128] = codes
        out[part, 0, 128:] = jnp.broadcast_to(slots[b : b + 1], (owners, lanes))
    put = pltpu.make_async_copy(out, out_hbm, sems.at[2])
    put.start()
    put.wait()


def leaving_ids(order, ids, owners):
    hashes, users, length = ids.shape
    hbm = pl.BlockSpec(memory_space=pltpu.HBM)
    free = pl.BlockSpec(memory_space=pl.ANY)
    shape = (users * owners, 1, 384)
    return pl.pallas_call(
        ids_kernel,
        out_shape=jax.ShapeDtypeStruct(shape, jnp.int32),
        in_specs=[hbm, hbm],
        out_specs=free,
        scratch_shapes=[
            pltpu.SMEM((users,), jnp.int32),
            pltpu.VMEM(ids.shape, jnp.int32),
            pltpu.VMEM((users, 256), jnp.int32),
            pltpu.VMEM(shape, jnp.int32),
            pltpu.SemaphoreType.DMA((3,)),
        ],
        compiler_params=pltpu.CompilerParams(vmem_limit_bytes=60 * MIB),
        name="leaving_ids",
    )(order, ids)


def serve_kernel(got_hbm, table_hbm, *refs):
    outs, (codes, raw, wide, stages, out, sems) = refs[:CHUNKS], refs[CHUNKS:]
    hashes, rows, width = table_hbm.shape
    tiles = width // 128
    _, requesters, half, _ = out.shape
    half_users = half // PER
    parts = 2 * hashes
    size = rows // 2
    get_codes = pltpu.make_async_copy(got_hbm.at[:, 0, pl.ds(0, 128)], codes, sems.at[parts])
    places = [(i // 2, (i % 2) * size) for i in range(parts)]
    copies = [
        pltpu.make_async_copy(
            table_hbm.at[h, pl.ds(first, size)], raw.at[h, pl.ds(first, size)], sems.at[i]
        )
        for i, (h, first) in enumerate(places)
    ]
    copies[0].start()
    get_codes.start()
    for copy in copies[1:]:
        copy.start()
    for i, (h, first) in enumerate(places):
        copies[i].wait()

        @pl.loop(0, size // 64)
        def _(g):
            for q in range(4):
                at = pl.multiple_of(first + g * 64 + q * 16, 16)
                for c in range(tiles):
                    both = raw[h, pl.ds(at, 16), c * 128 : (c + 1) * 128].astype(F32)
                    base = (h * rows + at) * tiles + c
                    wide[pl.ds(base, 8, stride=tiles), :] = both[:8]
                    wide[pl.ds(base + 8 * tiles, 8, stride=tiles), :] = both[8:]

    get_codes.wait()
    first_lane = lax.axis_index("batch") * PER

    def gather(side, t, part):
        for j in range(half_users):
            home = (part * half_users + j) * requesters + t
            for k in range(PER):
                row = codes[home, first_lane + k]
                slot = (j * PER + k) * tiles
                stages[side, slot : slot + tiles, :] = wide[
                    pl.ds(pl.multiple_of(row * tiles, tiles), tiles), :
                ]

    def pack(side, t, part):
        for g in range(half // 16):
            for c in range(tiles):
                base = g * 16 * tiles + c
                upper = stages[side, pl.ds(base, 8, stride=tiles), :]
                lower = stages[side, pl.ds(base + 8 * tiles, 8, stride=tiles), :]
                out[part, t, g * 16 : (g + 1) * 16, c * 128 : (c + 1) * 128] = jnp.concatenate(
                    [upper, lower], axis=0
                ).astype(BF)

    gather(0, 0, 0)

    @pl.loop(0, requesters)
    def _(t):
        gather(1, t, 1)
        pack(0, t, 0)

        @pl.when(t + 1 < requesters)
        def _():
            gather(0, t + 1, 0)

        pack(1, t, 1)

    puts = [
        pltpu.make_async_copy(out.at[i], outs[i], sems.at[parts + 1 + i]) for i in range(CHUNKS)
    ]
    for put in puts:
        put.start()
    for put in puts:
        put.wait()


def serve_rows(got, tables, requesters, per_chunk):
    hashes, rows, width = tables.shape
    tiles = width // 128
    shape = (requesters, per_chunk, width)
    hbm = pl.BlockSpec(memory_space=pltpu.HBM)
    free = pl.BlockSpec(memory_space=pl.ANY)
    return pl.pallas_call(
        serve_kernel,
        out_shape=[jax.ShapeDtypeStruct(shape, BF)] * CHUNKS,
        in_specs=[free, hbm],
        out_specs=[free, hbm],
        scratch_shapes=[
            pltpu.SMEM((got.shape[0], 128), jnp.int32),
            pltpu.VMEM(tables.shape, BF),
            pltpu.VMEM((hashes * rows * tiles, 128), F32),
            pltpu.VMEM((2, per_chunk * tiles, 128), F32),
            pltpu.VMEM((CHUNKS, *shape), BF),
            pltpu.SemaphoreType.DMA((2 * hashes + 1 + CHUNKS,)),
        ],
        compiler_params=pltpu.CompilerParams(vmem_limit_bytes=60 * MIB),
        name="serve_rows",
    )(got, tables)


def sigmoid(z):
    return 0.5 + 0.5 * jnp.tanh(0.5 * z)


def layer_kernel(chunk, *refs):
    len_hbm, got_hbm, fetched, cot_hbm, w_in_hbm, w_out_hbm = refs[:6]
    enc_hbm, grad_hbm, *refs = refs[7:] if chunk else refs[6:]
    lengths, got, cot, enc, grads, w_in, w_out, x_s, n_s, gate_s, *refs = refs
    dsilu_s, qkv_s, mixed_s, s_s, w_s, dw_s, dz_s, mask_s, sems = refs
    users, length, width = cot.shape
    tokens = users * length
    head = width // HEADS
    owners, per_chunk, _ = fetched.shape
    halves = 1
    half_users = users // halves
    half_tokens = tokens // halves
    half_rows = per_chunk // halves
    half_slots = owners * half_rows
    pair = 2 * length
    mine = lax.axis_index("table")
    our_users = pl.ds(chunk * users, users)

    def fetch(i, src, dst):
        copy = pltpu.make_async_copy(src, dst, sems.at[i])
        copy.start()
        return copy

    get_len = fetch(0, len_hbm, lengths)
    get_slots = [
        fetch(1 + j, got_hbm.at[pl.ds((chunk * users + j) * owners + mine, 1)], got.at[pl.ds(j, 1)])
        for j in range(users)
    ]
    sem_at = 1 + users
    get_w = {
        c: fetch(
            sem_at + c, w_in_hbm.at[0, :, pl.ds(c * width, width)], w_in.at[:, pl.ds(c * width, width)]
        )
        for c in PARTS_ORDER
    }
    sem_at += 4
    get_w_out = fetch(sem_at, w_out_hbm.at[0], w_out)
    get_cot = fetch(sem_at + 1, cot_hbm.at[our_users], cot)
    sem_at += 2

    get_len.wait()
    for copy in get_slots:
        copy.wait()
    slot_rows, slot_cols = [], []
    for i in range(halves):
        rows_of = []
        for h in range(3):
            packed = jnp.concatenate(
                [
                    got[i * half_users + j, :, 128 + h * length : 128 + (h + 1) * length]
                    for j in range(half_users)
                ],
                axis=1,
            )
            rows_of.append(
                lax.shift_right_logical(packed, 4) * half_rows
                + lax.div(iota((1, half_tokens), 1), length) * PER
                + (packed & 15)
            )
        stacked = jnp.concatenate(rows_of + [jnp.zeros((5, half_tokens), jnp.int32)], axis=0)
        slot_rows.append(rows_of)
        slot_cols.append(stacked.astype(F32).T.astype(jnp.int32))
    picks = []
    for i in range(halves):
        lane = iota((half_tokens, half_slots), 1)
        pick = (lane == slot_cols[i][:, 0:1]) | (lane == slot_cols[i][:, 1:2])
        pick = pick | (lane == slot_cols[i][:, 2:3])
        picks.append(jnp.where(pick, 1.0, 0.0).astype(BF))

    token_user = lax.div(iota((tokens, 1), 0), length)
    token_pos = iota((tokens, 1), 0) - token_user * length
    token_len = jnp.zeros((tokens, 1), jnp.int32)
    for u in range(users):
        token_len = jnp.where(token_user == u, lengths[chunk * users + u], token_len)
    live = jnp.where(token_pos < token_len, 1.0, 0.0).astype(F32)
    key = iota((tokens, pair), 1)
    query = iota((tokens, pair), 0)
    same = lax.div(key, length) == lax.rem(lax.div(query, length), 2)
    causal = lax.rem(key, length) <= lax.rem(query, length)
    mask_s[...] = jnp.where(same & causal, 1.0, 0.0) * live

    for i in range(halves):
        rows = slice(i * half_tokens, (i + 1) * half_tokens)
        block = fetched[:, i * half_rows : (i + 1) * half_rows, :].reshape(half_slots, width)
        x_s[rows] = dot(picks[i], block).astype(BF).astype(F32)
    x = x_s[...]
    mean = jnp.mean(x, axis=1, keepdims=True)
    centered = x - mean
    rstd = lax.rsqrt(jnp.mean(centered * centered, axis=1, keepdims=True) + EPS)
    n_s[...] = (centered * rstd).astype(BF)

    step = STEP
    for c in PARTS_ORDER:
        get_w[c].wait()
        for i in range(width // step):
            cols = slice(i * step, (i + 1) * step)
            z = dot(n_s[...], w_in[:, c * width + i * step : c * width + (i + 1) * step])
            sig = sigmoid(z)
            out = z * sig
            dsilu_s[c, :, cols] = sig + out * (1.0 - sig)
            if c == 0:
                gate_s[:, cols] = out
            else:
                qkv_s[c - 1, :, cols] = out.astype(BF)

    scale = head ** (-0.5)
    blocks = [
        (slice(p * pair, (p + 1) * pair), slice(h * head, (h + 1) * head))
        for h in range(HEADS)
        for p in range(tokens // pair)
    ]
    for at in blocks:
        s_s[at] = dot(qkv_s[(1, *at)], qkv_s[(2, *at)], NT)
    mask = mask_s[...]
    for h in range(HEADS):
        cols = slice(h * head, (h + 1) * head)
        s = s_s[:, cols] * scale
        sig = sigmoid(s)
        out = s * sig
        w_s[:, cols] = (out * mask).astype(BF)
        dw_s[:, cols] = (sig + out * (1.0 - sig)) * (mask * scale)
    for at in blocks:
        mixed_s[at] = dot(w_s[at], qkv_s[(0, *at)])

    mixed = mixed_s[...]
    mean2 = jnp.mean(mixed, axis=1, keepdims=True)
    centered2 = mixed - mean2
    rstd2 = lax.rsqrt(jnp.mean(centered2 * centered2, axis=1, keepdims=True) + EPS)
    hat = centered2 * rstd2
    gate = gate_s[...]
    gated = (hat * gate).astype(BF)
    get_w_out.wait()
    out = (x_s[...] + dot(gated, w_out[...])) * live
    enc[...] = out.astype(BF).reshape(users, length, width)
    send_enc = fetch(sem_at, enc, enc_hbm.at[our_users])
    sem_at += 1

    get_cot.wait()
    g = cot[...].reshape(tokens, width).astype(F32) * live
    dgated = dot(g.astype(BF), w_out[...], NT).astype(BF).astype(F32)
    dz_s[0] = (dgated * hat * dsilu_s[0]).astype(BF)
    dhat = dgated * gate
    dmixed = rstd2 * (
        dhat
        - jnp.mean(dhat, axis=1, keepdims=True)
        - hat * jnp.mean(dhat * hat, axis=1, keepdims=True)
    )
    n_s[...] = dmixed.astype(BF)
    for at in blocks:
        s_s[at] = dot(n_s[at], qkv_s[(0, *at)], NT)
    for at in blocks:
        dv = dot(w_s[at], n_s[at], TN).astype(BF).astype(F32)
        dz_s[(1, *at)] = (dv * dsilu_s[(1, *at)]).astype(BF)
    for h in range(HEADS):
        cols = slice(h * head, (h + 1) * head)
        w_s[:, cols] = (s_s[:, cols].astype(BF).astype(F32) * dw_s[:, cols]).astype(BF)
    for at in blocks:
        dq = dot(w_s[at], qkv_s[(2, *at)]).astype(BF).astype(F32)
        dz_s[(2, *at)] = (dq * dsilu_s[(2, *at)]).astype(BF)
    for at in blocks:
        dk = dot(w_s[at], qkv_s[(1, *at)], TN).astype(BF).astype(F32)
        dz_s[(3, *at)] = (dk * dsilu_s[(3, *at)]).astype(BF)

    for i in range(width // step):
        cols = slice(i * step, (i + 1) * step)
        dn = dot(dz_s[0], w_in[cols, :width], NT)
        for c in range(1, 4):
            dn = dn + dot(dz_s[c], w_in[cols, c * width : (c + 1) * width], NT)
        mixed_s[:, cols] = dn

    dn = mixed_s[...].astype(BF).astype(F32)
    xhat = (x_s[...] - mean) * rstd
    dx = rstd * (
        dn
        - jnp.mean(dn, axis=1, keepdims=True)
        - xhat * jnp.mean(dn * xhat, axis=1, keepdims=True)
    )
    n_s[...] = (dx + g).astype(BF)
    puts = []
    for i in range(halves):
        sub = iota((half_slots, half_tokens), 0)
        put = (sub == slot_rows[i][0]) | (sub == slot_rows[i][1]) | (sub == slot_rows[i][2])
        puts.append(jnp.where(put, 1.0, 0.0).astype(BF))
    ranks = grads.shape[0]
    copies = [send_enc]
    for b in range(0, ranks, 2):
        cols = slice(b * 128, (b + 2) * 128)
        for i in range(halves):
            rows = slice(i * half_tokens, (i + 1) * half_tokens)
            two = dot(puts[i], n_s[rows, cols]).astype(BF)
            for r in range(2):
                grads[b + r, :, i * half_rows : (i + 1) * half_rows, :] = two[
                    :, r * 128 : (r + 1) * 128
                ].reshape(owners, half_rows, 128)
        copies.append(fetch(sem_at, grads.at[pl.ds(b, 2)], grad_hbm.at[pl.ds(b, 2)]))
        sem_at += 1
    for copy in copies:
        copy.wait()


def layer(chunk, lengths, got, fetched, cot, w_in, w_out, batch_ranks, prev):
    owners, per_chunk, width = fetched.shape
    all_users, length, _ = cot.shape
    users = all_users // CHUNKS
    tokens = users * length
    ours = (users, length, width)
    grad_shape = (batch_ranks, owners, per_chunk, width // batch_ranks)
    hbm = pl.BlockSpec(memory_space=pltpu.HBM)
    free = pl.BlockSpec(memory_space=pl.ANY)
    vmem = pl.BlockSpec(memory_space=pltpu.VMEM)
    args = (lengths, got, fetched, cot, w_in, w_out) + ((prev,) if chunk else ())
    return pl.pallas_call(
        functools.partial(layer_kernel, chunk),
        out_shape=[
            jax.ShapeDtypeStruct(cot.shape, BF),
            jax.ShapeDtypeStruct(grad_shape, BF),
        ],
        in_specs=[hbm, free, vmem, hbm, hbm, hbm, hbm][: len(args)],
        out_specs=[hbm, hbm],
        input_output_aliases={6: 0} if chunk else {},
        scratch_shapes=[
            pltpu.SMEM((all_users,), jnp.int32),
            pltpu.VMEM((users, 1, got.shape[2]), jnp.int32),
            pltpu.VMEM(ours, BF),
            pltpu.VMEM(ours, BF),
            pltpu.VMEM(grad_shape, BF),
            pltpu.VMEM((width, 4 * width), BF),
            pltpu.VMEM((width, width), BF),
            pltpu.VMEM((tokens, width), F32),
            pltpu.VMEM((tokens, width), BF),
            pltpu.VMEM((tokens, width), F32),
            pltpu.VMEM((4, tokens, width), F32),
            pltpu.VMEM((3, tokens, width), BF),
            pltpu.VMEM((tokens, width), F32),
            pltpu.VMEM((tokens, width), F32),
            pltpu.VMEM((tokens, width), BF),
            pltpu.VMEM((tokens, width), F32),
            pltpu.VMEM((4, tokens, width), BF),
            pltpu.VMEM((tokens, 2 * length), F32),
            pltpu.SemaphoreType.DMA((10 + users + batch_ranks // 2,)),
        ],
        compiler_params=pltpu.CompilerParams(vmem_limit_bytes=LAYER_VMEM),
        cost_estimate=COST,
        name="layer",
    )(*args)


def collect_kernel(chunk, got_hbm, rows, *refs):
    prev_hbm = refs[0] if chunk else None
    out_hbm, got, codes, wide, hits, out, prev, sems = refs[1 if chunk else 0 :]
    senders, per_sender, cols = rows.shape
    ranks = senders // OWNERS
    users = per_sender // PER
    groups, depth = codes.shape
    group = senders // groups
    parts = wide.shape[1] // cols
    height = out.shape[0] // parts
    get_codes = pltpu.make_async_copy(got_hbm.at[:, :, pl.ds(0, 128)], got, sems.at[0])
    get_codes.start()
    if chunk:
        get_prev = pltpu.make_async_copy(prev_hbm, prev, sems.at[1])
        get_prev.start()
    get_codes.wait()
    lane = iota((OWNERS, 128), 1)
    for b in range(ranks):
        line = jnp.zeros((OWNERS, 128), jnp.int32)
        for j in range(users):
            home = (chunk * users + j) * OWNERS
            block = got[home : home + OWNERS, 0, :]
            moved = pltpu.roll(block, ((j - b) * PER) % 128, 1)
            line = jnp.where((lane >= j * PER) & (lane < (j + 1) * PER), moved, line)
        for t in range(OWNERS):
            sender = b * OWNERS + t
            first = (sender % group) * per_sender
            codes[sender // group : sender // group + 1, first : first + per_sender] = line[
                t : t + 1, :per_sender
            ]
    part_cols = lax.div(codes[...], height).astype(F32).T.astype(jnp.int32)
    for s in range(groups):
        inside = lax.rem(codes[s : s + 1, :], height)
        for q in range(height // 128):
            near = jnp.clip(inside - 128 * q, -1, 128).astype(F32).astype(BF)
            row = iota((128, depth), 0).astype(F32).astype(BF)
            hits[q * 128 : (q + 1) * 128, s * depth : (s + 1) * depth] = jnp.where(
                row == near, jnp.ones((), BF), jnp.zeros((), BF)
            )
        block = rows[s * group : (s + 1) * group].reshape(depth, cols)
        for p in range(parts):
            here = part_cols[:, s : s + 1] == p
            wide[s * depth : (s + 1) * depth, p * cols : (p + 1) * cols] = jnp.where(
                here, block, jnp.zeros_like(block)
            )
    if chunk:
        get_prev.wait()
    acc = dot(hits[...], wide[...])
    puts = []
    for p in range(parts):
        at = slice(p * height, (p + 1) * height)
        part = acc[:, p * cols : (p + 1) * cols]
        out[at, :] = part + prev[at, :] if chunk else part
        puts.append(pltpu.make_async_copy(out.at[at], out_hbm.at[at], sems.at[2 + p]))
        puts[-1].start()
    for put in puts:
        put.wait()


def collect(chunk, got, rows, prev, total):
    args = (got, rows) + ((prev,) if chunk else ())
    senders, per_sender, cols = rows.shape
    hbm = pl.BlockSpec(memory_space=pltpu.HBM)
    free = pl.BlockSpec(memory_space=pl.ANY)
    vmem = pl.BlockSpec(memory_space=pltpu.VMEM)
    return pl.pallas_call(
        functools.partial(collect_kernel, chunk),
        out_shape=jax.ShapeDtypeStruct((total, cols), F32),
        in_specs=[free, vmem, hbm][: len(args)],
        out_specs=hbm,
        scratch_shapes=[
            pltpu.VMEM((got.shape[0], 1, 128), jnp.int32),
            pltpu.VMEM((senders // GROUP, GROUP * per_sender), jnp.int32),
            pltpu.VMEM((senders * per_sender, PARTS * cols), BF),
            pltpu.VMEM((total // PARTS, senders * per_sender), BF),
            pltpu.VMEM((total, cols), F32),
            pltpu.VMEM((total, cols), F32),
            pltpu.SemaphoreType.DMA((2 + PARTS,)),
        ],
        compiler_params=pltpu.CompilerParams(vmem_limit_bytes=COLLECT_VMEM),
        cost_estimate=COST,
        name="collect",
    )(*args)


def body(item_rows, send_order, user_lengths, tables, w_in, w_out, out_grad):
    batch_ranks = lax.axis_size("batch")
    table_ranks = lax.axis_size("table")
    users, length, hashes = item_rows.shape
    rows_local = tables.shape[1]
    both = ("batch", "table")
    per_chunk = users // CHUNKS * PER

    leaving = leaving_ids(send_order, item_rows.transpose(2, 0, 1), table_ranks)
    got = lax.all_to_all(leaving, both, 0, 0, tiled=True)
    served = serve_rows(got, tables, table_ranks, per_chunk)
    encoded, total, returned = None, None, []
    for c in range(CHUNKS):
        fetched = lax.all_to_all(served[c], "table", 0, 0, tiled=True)
        encoded, grads = layer(
            c, user_lengths, got, fetched, out_grad, w_in, w_out, batch_ranks, encoded
        )
        grads = grads.reshape(batch_ranks * table_ranks, per_chunk, -1)
        returned.append(lax.all_to_all(grads, both, 0, 0, tiled=True))
    for c in range(CHUNKS):
        total = collect(c, got, returned[c], total, hashes * rows_local)
    return encoded, total.reshape(hashes, rows_local, -1)


def solution(mesh):
    in_specs = (
        P(("batch", "table"), None, None),
        P(("batch", "table")),
        P(("batch", "table")),
        P(None, "table", None),
        P(),
        P(),
        P(("batch", "table"), None, None),
    )
    out_specs = (P(("batch", "table"), None, None), P(None, "table", "batch"))
    return jax.shard_map(body, mesh=mesh, in_specs=in_specs, out_specs=out_specs, check_vma=False)
```

```python
import functools

import jax
import jax.numpy as jnp
from jax import lax
from jax.experimental import pallas as pl
from jax.experimental.pallas import tpu as pltpu
from jax.sharding import PartitionSpec as P

HEADS = 8
PER = 12
EPS = 1e-05
BF = jnp.bfloat16
F32 = jnp.float32
NT = (((1,), (1,)), ((), ()))
NN = (((1,), (0,)), ((), ()))
TN = (((0,), (0,)), ((), ()))
CHUNKS = 2
MIB = 1024 * 1024
LAYER_VMEM = 49 * MIB
COLLECT_VMEM = 52 * MIB
PARTS = 4
OWNERS = 16
GROUP = 16
COST = pl.CostEstimate(flops=12_000_000_000, bytes_accessed=20_000_000, transcendentals=0)
PARTS_ORDER = (2, 3, 1, 0)
STEP = 256


def dot(a, b, dims=NN):
    return lax.dot_general(a, b, dims, preferred_element_type=F32)


def iota(shape, dim):
    return lax.broadcasted_iota(jnp.int32, shape, dim)


def ids_kernel(order_hbm, ids_hbm, out_hbm, order, raw, ids_scr, out, sems):
    hashes, users, length = raw.shape
    owners = out.shape[0] // users
    get_order = pltpu.make_async_copy(order_hbm, order, sems.at[0])
    get_ids = pltpu.make_async_copy(ids_hbm, raw, sems.at[1])
    get_order.start()
    get_ids.start()
    ids_scr[...] = jnp.full(ids_scr.shape, -1, jnp.int32)
    get_order.wait()
    get_ids.wait()
    for b in range(users):
        user = order[b]
        for h in range(hashes):
            ids_scr[b : b + 1, h * length : (h + 1) * length] = raw[h, pl.ds(user, 1), :]
    ids = ids_scr[...]
    lanes = ids.shape[1]
    owner = lax.shift_right_arithmetic(ids, 10)
    hash_of = lax.div(iota(ids.shape, 1), length)
    code = (ids & 1023) + 1024 * hash_of
    high = (lax.shift_right_logical(code, 6)).astype(F32)
    low = (code & 63).astype(F32)
    hits = [jnp.where(owner == o, 1.0, 0.0).astype(F32) for o in range(owners)]
    before = jnp.where(iota((lanes, lanes), 0) < iota((lanes, lanes), 1), 1.0, 0.0).astype(BF)
    prefix = dot(jnp.concatenate(hits, axis=0).astype(BF), before)
    rank = jnp.zeros(ids.shape, F32)
    for o in range(owners):
        rank = rank + hits[o] * prefix[o * users : (o + 1) * users]
    rank = rank.astype(jnp.int32)
    total = jnp.zeros((2 * owners, 128), F32)
    for b in range(users):
        hit = iota((owners, lanes), 0) == owner[b : b + 1]
        left = jnp.concatenate(
            [jnp.where(hit, high[b : b + 1], 0.0), jnp.where(hit, low[b : b + 1], 0.0)], axis=0
        ).astype(BF)
        right = jnp.where(iota((128, lanes), 0) == rank[b : b + 1] + PER * b, 1.0, 0.0).astype(BF)
        total = total + dot(left, right, NT)
    codes = (total[:owners] * 64.0 + total[owners:]).astype(jnp.int32)
    slots = owner * 16 + rank
    for b in range(users):
        part = pl.ds(b * owners, owners)
        out[part, 0, :128] = codes
        out[part, 0, 128:] = jnp.broadcast_to(slots[b : b + 1], (owners, lanes))
    put = pltpu.make_async_copy(out, out_hbm, sems.at[2])
    put.start()
    put.wait()


def leaving_ids(order, ids, owners):
    hashes, users, length = ids.shape
    hbm = pl.BlockSpec(memory_space=pltpu.HBM)
    free = pl.BlockSpec(memory_space=pl.ANY)
    shape = (users * owners, 1, 384)
    return pl.pallas_call(
        ids_kernel,
        out_shape=jax.ShapeDtypeStruct(shape, jnp.int32),
        in_specs=[hbm, hbm],
        out_specs=free,
        scratch_shapes=[
            pltpu.SMEM((users,), jnp.int32),
            pltpu.VMEM(ids.shape, jnp.int32),
            pltpu.VMEM((users, 256), jnp.int32),
            pltpu.VMEM(shape, jnp.int32),
            pltpu.SemaphoreType.DMA((3,)),
        ],
        compiler_params=pltpu.CompilerParams(vmem_limit_bytes=60 * MIB),
        name="leaving_ids",
    )(order, ids)


def serve_kernel(got_hbm, table_hbm, *refs):
    outs, (codes, raw, wide, stages, out, sems) = refs[:CHUNKS], refs[CHUNKS:]
    hashes, rows, width = table_hbm.shape
    tiles = width // 128
    _, requesters, half, _ = out.shape
    half_users = half // PER
    parts = 2 * hashes
    size = rows // 2
    get_codes = pltpu.make_async_copy(got_hbm.at[:, 0, pl.ds(0, 128)], codes, sems.at[parts])
    places = [(i // 2, (i % 2) * size) for i in range(parts)]
    copies = [
        pltpu.make_async_copy(
            table_hbm.at[h, pl.ds(first, size)], raw.at[h, pl.ds(first, size)], sems.at[i]
        )
        for i, (h, first) in enumerate(places)
    ]
    copies[0].start()
    get_codes.start()
    for copy in copies[1:]:
        copy.start()
    for i, (h, first) in enumerate(places):
        copies[i].wait()

        @pl.loop(0, size // 64)
        def _(g):
            for q in range(4):
                at = pl.multiple_of(first + g * 64 + q * 16, 16)
                for c in range(tiles):
                    both = raw[h, pl.ds(at, 16), c * 128 : (c + 1) * 128].astype(F32)
                    base = (h * rows + at) * tiles + c
                    wide[pl.ds(base, 8, stride=tiles), :] = both[:8]
                    wide[pl.ds(base + 8 * tiles, 8, stride=tiles), :] = both[8:]

    get_codes.wait()
    first_lane = lax.axis_index("batch") * PER

    def gather(side, t, part):
        for j in range(half_users):
            home = (part * half_users + j) * requesters + t
            for k in range(PER):
                row = codes[home, first_lane + k]
                slot = (j * PER + k) * tiles
                stages[side, slot : slot + tiles, :] = wide[
                    pl.ds(pl.multiple_of(row * tiles, tiles), tiles), :
                ]

    def pack(side, t, part):
        for g in range(half // 16):
            for c in range(tiles):
                base = g * 16 * tiles + c
                upper = stages[side, pl.ds(base, 8, stride=tiles), :]
                lower = stages[side, pl.ds(base + 8 * tiles, 8, stride=tiles), :]
                out[part, t, g * 16 : (g + 1) * 16, c * 128 : (c + 1) * 128] = jnp.concatenate(
                    [upper, lower], axis=0
                ).astype(BF)

    gather(0, 0, 0)

    @pl.loop(0, requesters)
    def _(t):
        gather(1, t, 1)
        pack(0, t, 0)

        @pl.when(t + 1 < requesters)
        def _():
            gather(0, t + 1, 0)

        pack(1, t, 1)
        for i in range(CHUNKS):
            pltpu.make_async_copy(out.at[i, t], outs[i].at[t], sems.at[parts + 1 + i]).start()

    puts = [
        pltpu.make_async_copy(out.at[i], outs[i], sems.at[parts + 1 + i]) for i in range(CHUNKS)
    ]
    for put in puts:
        put.wait()


def serve_rows(got, tables, requesters, per_chunk):
    hashes, rows, width = tables.shape
    tiles = width // 128
    shape = (requesters, per_chunk, width)
    hbm = pl.BlockSpec(memory_space=pltpu.HBM)
    free = pl.BlockSpec(memory_space=pl.ANY)
    return pl.pallas_call(
        serve_kernel,
        out_shape=[jax.ShapeDtypeStruct(shape, BF)] * CHUNKS,
        in_specs=[free, hbm],
        out_specs=[free, hbm],
        scratch_shapes=[
            pltpu.SMEM((got.shape[0], 128), jnp.int32),
            pltpu.VMEM(tables.shape, BF),
            pltpu.VMEM((hashes * rows * tiles, 128), F32),
            pltpu.VMEM((2, per_chunk * tiles, 128), F32),
            pltpu.VMEM((CHUNKS, *shape), BF),
            pltpu.SemaphoreType.DMA((2 * hashes + 1 + CHUNKS,)),
        ],
        compiler_params=pltpu.CompilerParams(vmem_limit_bytes=60 * MIB),
        name="serve_rows",
    )(got, tables)


def sigmoid(z):
    return 0.5 + 0.5 * jnp.tanh(0.5 * z)


def layer_kernel(chunk, *refs):
    len_hbm, got_hbm, fetched, cot_hbm, w_in_hbm, w_out_hbm = refs[:6]
    enc_hbm, grad_hbm, *refs = refs[7:] if chunk else refs[6:]
    lengths, got, cot, enc, grads, w_in, w_out, x_s, n_s, gate_s, *refs = refs
    dsilu_s, qkv_s, mixed_s, s_s, w_s, dw_s, dz_s, mask_s, sems = refs
    users, length, width = cot.shape
    tokens = users * length
    head = width // HEADS
    owners, per_chunk, _ = fetched.shape
    halves = 1
    half_users = users // halves
    half_tokens = tokens // halves
    half_rows = per_chunk // halves
    half_slots = owners * half_rows
    pair = 2 * length
    mine = lax.axis_index("table")
    our_users = pl.ds(chunk * users, users)

    def fetch(i, src, dst):
        copy = pltpu.make_async_copy(src, dst, sems.at[i])
        copy.start()
        return copy

    get_len = fetch(0, len_hbm, lengths)
    get_slots = [
        fetch(1 + j, got_hbm.at[pl.ds((chunk * users + j) * owners + mine, 1)], got.at[pl.ds(j, 1)])
        for j in range(users)
    ]
    sem_at = 1 + users
    get_w = {
        c: fetch(
            sem_at + c, w_in_hbm.at[0, :, pl.ds(c * width, width)], w_in.at[:, pl.ds(c * width, width)]
        )
        for c in PARTS_ORDER
    }
    sem_at += 4
    get_w_out = fetch(sem_at, w_out_hbm.at[0], w_out)
    get_cot = fetch(sem_at + 1, cot_hbm.at[our_users], cot)
    sem_at += 2

    get_len.wait()
    for copy in get_slots:
        copy.wait()
    slot_rows, slot_cols = [], []
    for i in range(halves):
        rows_of = []
        for h in range(3):
            packed = jnp.concatenate(
                [
                    got[i * half_users + j, :, 128 + h * length : 128 + (h + 1) * length]
                    for j in range(half_users)
                ],
                axis=1,
            )
            rows_of.append(
                lax.shift_right_logical(packed, 4) * half_rows
                + lax.div(iota((1, half_tokens), 1), length) * PER
                + (packed & 15)
            )
        stacked = jnp.concatenate(rows_of + [jnp.zeros((5, half_tokens), jnp.int32)], axis=0)
        slot_rows.append(rows_of)
        slot_cols.append(stacked.astype(F32).T.astype(jnp.int32))
    picks = []
    for i in range(halves):
        lane = iota((half_tokens, half_slots), 1)
        pick = (lane == slot_cols[i][:, 0:1]) | (lane == slot_cols[i][:, 1:2])
        pick = pick | (lane == slot_cols[i][:, 2:3])
        picks.append(jnp.where(pick, 1.0, 0.0).astype(BF))

    token_user = lax.div(iota((tokens, 1), 0), length)
    token_pos = iota((tokens, 1), 0) - token_user * length
    token_len = jnp.zeros((tokens, 1), jnp.int32)
    for u in range(users):
        token_len = jnp.where(token_user == u, lengths[chunk * users + u], token_len)
    live = jnp.where(token_pos < token_len, 1.0, 0.0).astype(F32)
    key = iota((tokens, pair), 1)
    query = iota((tokens, pair), 0)
    same = lax.div(key, length) == lax.rem(lax.div(query, length), 2)
    causal = lax.rem(key, length) <= lax.rem(query, length)
    mask_s[...] = jnp.where(same & causal, 1.0, 0.0) * live

    for i in range(halves):
        rows = slice(i * half_tokens, (i + 1) * half_tokens)
        block = fetched[:, i * half_rows : (i + 1) * half_rows, :].reshape(half_slots, width)
        x_s[rows] = dot(picks[i], block).astype(BF).astype(F32)
    x = x_s[...]
    mean = jnp.mean(x, axis=1, keepdims=True)
    centered = x - mean
    rstd = lax.rsqrt(jnp.mean(centered * centered, axis=1, keepdims=True) + EPS)
    n_s[...] = (centered * rstd).astype(BF)

    step = STEP
    for c in PARTS_ORDER:
        get_w[c].wait()

        @pl.loop(0, width // step)
        def _(i, c=c):
            cols = pl.ds(pl.multiple_of(i * step, step), step)
            z = dot(n_s[...], w_in[:, pl.ds(pl.multiple_of(c * width + i * step, step), step)])
            sig = sigmoid(z)
            out = z * sig
            dsilu_s[c, :, cols] = sig + out * (1.0 - sig)
            if c == 0:
                gate_s[:, cols] = out
            else:
                qkv_s[c - 1, :, cols] = out.astype(BF)

    scale = head ** (-0.5)
    blocks = [
        (slice(p * pair, (p + 1) * pair), slice(h * head, (h + 1) * head))
        for h in range(HEADS)
        for p in range(tokens // pair)
    ]
    for at in blocks:
        s_s[at] = dot(qkv_s[(1, *at)], qkv_s[(2, *at)], NT)
    mask = mask_s[...]
    for h in range(HEADS):
        cols = slice(h * head, (h + 1) * head)
        s = s_s[:, cols] * scale
        sig = sigmoid(s)
        out = s * sig
        w_s[:, cols] = (out * mask).astype(BF)
        dw_s[:, cols] = (sig + out * (1.0 - sig)) * (mask * scale)
    for at in blocks:
        mixed_s[at] = dot(w_s[at], qkv_s[(0, *at)])

    mixed = mixed_s[...]
    mean2 = jnp.mean(mixed, axis=1, keepdims=True)
    centered2 = mixed - mean2
    rstd2 = lax.rsqrt(jnp.mean(centered2 * centered2, axis=1, keepdims=True) + EPS)
    hat = centered2 * rstd2
    gate = gate_s[...]
    gated = (hat * gate).astype(BF)
    get_w_out.wait()
    out = (x_s[...] + dot(gated, w_out[...])) * live
    enc[...] = out.astype(BF).reshape(users, length, width)
    send_enc = fetch(sem_at, enc, enc_hbm.at[our_users])
    sem_at += 1

    get_cot.wait()
    g = cot[...].reshape(tokens, width).astype(F32) * live
    dgated = dot(g.astype(BF), w_out[...], NT).astype(BF).astype(F32)
    dz_s[0] = (dgated * hat * dsilu_s[0]).astype(BF)
    dhat = dgated * gate
    dmixed = rstd2 * (
        dhat
        - jnp.mean(dhat, axis=1, keepdims=True)
        - hat * jnp.mean(dhat * hat, axis=1, keepdims=True)
    )
    n_s[...] = dmixed.astype(BF)
    for at in blocks:
        s_s[at] = dot(n_s[at], qkv_s[(0, *at)], NT)
    for at in blocks:
        dv = dot(w_s[at], n_s[at], TN).astype(BF).astype(F32)
        dz_s[(1, *at)] = (dv * dsilu_s[(1, *at)]).astype(BF)
    for h in range(HEADS):
        cols = slice(h * head, (h + 1) * head)
        w_s[:, cols] = (s_s[:, cols].astype(BF).astype(F32) * dw_s[:, cols]).astype(BF)
    for at in blocks:
        dq = dot(w_s[at], qkv_s[(2, *at)]).astype(BF).astype(F32)
        dz_s[(2, *at)] = (dq * dsilu_s[(2, *at)]).astype(BF)
    for at in blocks:
        dk = dot(w_s[at], qkv_s[(1, *at)], TN).astype(BF).astype(F32)
        dz_s[(3, *at)] = (dk * dsilu_s[(3, *at)]).astype(BF)

    @pl.loop(0, width // step)
    def _(i):
        cols = pl.ds(pl.multiple_of(i * step, step), step)
        dn = dot(dz_s[0], w_in[cols, :width], NT)
        for c in range(1, 4):
            dn = dn + dot(dz_s[c], w_in[cols, c * width : (c + 1) * width], NT)
        mixed_s[:, cols] = dn

    dn = mixed_s[...].astype(BF).astype(F32)
    xhat = (x_s[...] - mean) * rstd
    dx = rstd * (
        dn
        - jnp.mean(dn, axis=1, keepdims=True)
        - xhat * jnp.mean(dn * xhat, axis=1, keepdims=True)
    )
    n_s[...] = (dx + g).astype(BF)
    puts = []
    for i in range(halves):
        sub = iota((half_slots, half_tokens), 0)
        put = (sub == slot_rows[i][0]) | (sub == slot_rows[i][1]) | (sub == slot_rows[i][2])
        puts.append(jnp.where(put, 1.0, 0.0).astype(BF))
    ranks = grads.shape[0]
    copies = [send_enc]
    for b in range(0, ranks, 2):
        cols = slice(b * 128, (b + 2) * 128)
        for i in range(halves):
            rows = slice(i * half_tokens, (i + 1) * half_tokens)
            two = dot(puts[i], n_s[rows, cols]).astype(BF)
            for r in range(2):
                grads[b + r, :, i * half_rows : (i + 1) * half_rows, :] = two[
                    :, r * 128 : (r + 1) * 128
                ].reshape(owners, half_rows, 128)
        copies.append(fetch(sem_at, grads.at[pl.ds(b, 2)], grad_hbm.at[pl.ds(b, 2)]))
        sem_at += 1
    for copy in copies:
        copy.wait()


def layer(chunk, lengths, got, fetched, cot, w_in, w_out, batch_ranks, prev):
    owners, per_chunk, width = fetched.shape
    all_users, length, _ = cot.shape
    users = all_users // CHUNKS
    tokens = users * length
    ours = (users, length, width)
    grad_shape = (batch_ranks, owners, per_chunk, width // batch_ranks)
    hbm = pl.BlockSpec(memory_space=pltpu.HBM)
    free = pl.BlockSpec(memory_space=pl.ANY)
    vmem = pl.BlockSpec(memory_space=pltpu.VMEM)
    args = (lengths, got, fetched, cot, w_in, w_out) + ((prev,) if chunk else ())
    return pl.pallas_call(
        functools.partial(layer_kernel, chunk),
        out_shape=[
            jax.ShapeDtypeStruct(cot.shape, BF),
            jax.ShapeDtypeStruct(grad_shape, BF),
        ],
        in_specs=[hbm, free, vmem, hbm, hbm, hbm, hbm][: len(args)],
        out_specs=[hbm, hbm],
        input_output_aliases={6: 0} if chunk else {},
        scratch_shapes=[
            pltpu.SMEM((all_users,), jnp.int32),
            pltpu.VMEM((users, 1, got.shape[2]), jnp.int32),
            pltpu.VMEM(ours, BF),
            pltpu.VMEM(ours, BF),
            pltpu.VMEM(grad_shape, BF),
            pltpu.VMEM((width, 4 * width), BF),
            pltpu.VMEM((width, width), BF),
            pltpu.VMEM((tokens, width), F32),
            pltpu.VMEM((tokens, width), BF),
            pltpu.VMEM((tokens, width), F32),
            pltpu.VMEM((4, tokens, width), F32),
            pltpu.VMEM((3, tokens, width), BF),
            pltpu.VMEM((tokens, width), F32),
            pltpu.VMEM((tokens, width), F32),
            pltpu.VMEM((tokens, width), BF),
            pltpu.VMEM((tokens, width), F32),
            pltpu.VMEM((4, tokens, width), BF),
            pltpu.VMEM((tokens, 2 * length), F32),
            pltpu.SemaphoreType.DMA((10 + users + batch_ranks // 2,)),
        ],
        compiler_params=pltpu.CompilerParams(vmem_limit_bytes=LAYER_VMEM),
        cost_estimate=COST,
        name="layer",
    )(*args)


def collect_kernel(chunk, got_hbm, rows, *refs):
    prev_hbm = refs[0] if chunk else None
    out_hbm, got, codes, wide, hits, out, prev, sems = refs[1 if chunk else 0 :]
    senders, per_sender, cols = rows.shape
    ranks = senders // OWNERS
    users = per_sender // PER
    groups, depth = codes.shape
    group = senders // groups
    parts = wide.shape[1] // cols
    height = out.shape[0] // parts
    get_codes = pltpu.make_async_copy(got_hbm.at[:, :, pl.ds(0, 128)], got, sems.at[0])
    get_codes.start()
    if chunk:
        get_prev = pltpu.make_async_copy(prev_hbm, prev, sems.at[1])
        get_prev.start()
    get_codes.wait()
    if chunk:
        get_prev.wait()
    lane = iota((OWNERS, 128), 1)
    for b in range(ranks):
        line = jnp.zeros((OWNERS, 128), jnp.int32)
        for j in range(users):
            home = (chunk * users + j) * OWNERS
            block = got[home : home + OWNERS, 0, :]
            moved = pltpu.roll(block, ((j - b) * PER) % 128, 1)
            line = jnp.where((lane >= j * PER) & (lane < (j + 1) * PER), moved, line)
        for t in range(OWNERS):
            sender = b * OWNERS + t
            first = (sender % group) * per_sender
            codes[sender // group : sender // group + 1, first : first + per_sender] = line[
                t : t + 1, :per_sender
            ]
    part_cols = lax.div(codes[...], height).astype(F32).T.astype(jnp.int32)
    for s in range(groups):
        inside = lax.rem(codes[s : s + 1, :], height)
        for q in range(height // 128):
            near = jnp.clip(inside - 128 * q, -1, 128).astype(F32).astype(BF)
            row = iota((128, depth), 0).astype(F32).astype(BF)
            hits[q * 128 : (q + 1) * 128, s * depth : (s + 1) * depth] = jnp.where(
                row == near, jnp.ones((), BF), jnp.zeros((), BF)
            )
        block = rows[s * group : (s + 1) * group].reshape(depth, cols)
        for p in range(parts):
            here = part_cols[:, s : s + 1] == p
            wide[s * depth : (s + 1) * depth, p * cols : (p + 1) * cols] = jnp.where(
                here, block, jnp.zeros_like(block)
            )
    acc = dot(hits[...], wide[...])
    puts = []
    for p in range(parts):
        at = slice(p * height, (p + 1) * height)
        part = acc[:, p * cols : (p + 1) * cols]
        out[at, :] = part + prev[at, :] if chunk else part
        puts.append(pltpu.make_async_copy(out.at[at], out_hbm.at[at], sems.at[2 + p]))
        puts[-1].start()
    for put in puts:
        put.wait()


def collect(chunk, got, rows, prev, total):
    args = (got, rows) + ((prev,) if chunk else ())
    senders, per_sender, cols = rows.shape
    hbm = pl.BlockSpec(memory_space=pltpu.HBM)
    free = pl.BlockSpec(memory_space=pl.ANY)
    vmem = pl.BlockSpec(memory_space=pltpu.VMEM)
    return pl.pallas_call(
        functools.partial(collect_kernel, chunk),
        out_shape=jax.ShapeDtypeStruct((total, cols), F32),
        in_specs=[free, vmem, hbm][: len(args)],
        out_specs=hbm,
        scratch_shapes=[
            pltpu.VMEM((got.shape[0], 1, 128), jnp.int32),
            pltpu.VMEM((senders // GROUP, GROUP * per_sender), jnp.int32),
            pltpu.VMEM((senders * per_sender, PARTS * cols), BF),
            pltpu.VMEM((total // PARTS, senders * per_sender), BF),
            pltpu.VMEM((total, cols), F32),
            pltpu.VMEM((total, cols), F32),
            pltpu.SemaphoreType.DMA((2 + PARTS,)),
        ],
        compiler_params=pltpu.CompilerParams(vmem_limit_bytes=COLLECT_VMEM),
        cost_estimate=COST,
        name="collect",
    )(*args)


def body(item_rows, send_order, user_lengths, tables, w_in, w_out, out_grad):
    batch_ranks = lax.axis_size("batch")
    table_ranks = lax.axis_size("table")
    users, length, hashes = item_rows.shape
    rows_local = tables.shape[1]
    both = ("batch", "table")
    per_chunk = users // CHUNKS * PER

    leaving = leaving_ids(send_order, item_rows.transpose(2, 0, 1), table_ranks)
    got = lax.all_to_all(leaving, both, 0, 0, tiled=True)
    served = serve_rows(got, tables, table_ranks, per_chunk)
    encoded, total, returned = None, None, []
    for c in range(CHUNKS):
        fetched = lax.all_to_all(served[c], "table", 0, 0, tiled=True)
        encoded, grads = layer(
            c, user_lengths, got, fetched, out_grad, w_in, w_out, batch_ranks, encoded
        )
        grads = grads.reshape(batch_ranks * table_ranks, per_chunk, -1)
        returned.append(lax.all_to_all(grads, both, 0, 0, tiled=True))
    for c in range(CHUNKS):
        total = collect(c, got, returned[c], total, hashes * rows_local)
    return encoded, total.reshape(hashes, rows_local, -1)


def solution(mesh):
    in_specs = (
        P(("batch", "table"), None, None),
        P(("batch", "table")),
        P(("batch", "table")),
        P(None, "table", None),
        P(),
        P(),
        P(("batch", "table"), None, None),
    )
    out_specs = (P(("batch", "table"), None, None), P(None, "table", "batch"))
    return jax.shard_map(body, mesh=mesh, in_specs=in_specs, out_specs=out_specs, check_vma=False)
```

```python
import functools

import jax
import jax.numpy as jnp
from jax import lax
from jax.experimental import pallas as pl
from jax.experimental.pallas import tpu as pltpu
from jax.sharding import PartitionSpec as P

HEADS = 8
PER = 12
EPS = 1e-05
BF = jnp.bfloat16
F32 = jnp.float32
NT = (((1,), (1,)), ((), ()))
NN = (((1,), (0,)), ((), ()))
TN = (((0,), (0,)), ((), ()))
CHUNKS = 2
MIB = 1024 * 1024
LAYER_VMEM = 49 * MIB
SERVE_VMEM = 50 * MIB
COLLECT_VMEM = 52 * MIB
PARTS = 4
OWNERS = 16
GROUP = 16
COST = pl.CostEstimate(flops=12_000_000_000, bytes_accessed=20_000_000, transcendentals=0)
PARTS_ORDER = (2, 3, 1, 0)
STEP = 256


def dot(a, b, dims=NN):
    return lax.dot_general(a, b, dims, preferred_element_type=F32)


def iota(shape, dim):
    return lax.broadcasted_iota(jnp.int32, shape, dim)


def ids_kernel(order_hbm, ids_hbm, out_hbm, order, raw, ids_scr, out, sems):
    hashes, users, length = raw.shape
    owners = out.shape[0] // users
    get_order = pltpu.make_async_copy(order_hbm, order, sems.at[0])
    get_ids = pltpu.make_async_copy(ids_hbm, raw, sems.at[1])
    get_order.start()
    get_ids.start()
    ids_scr[...] = jnp.full(ids_scr.shape, -1, jnp.int32)
    get_order.wait()
    get_ids.wait()
    for b in range(users):
        user = order[b]
        for h in range(hashes):
            ids_scr[b : b + 1, h * length : (h + 1) * length] = raw[h, pl.ds(user, 1), :]
    ids = ids_scr[...]
    lanes = ids.shape[1]
    owner = lax.shift_right_arithmetic(ids, 10)
    hash_of = lax.div(iota(ids.shape, 1), length)
    code = (ids & 1023) + 1024 * hash_of
    high = (lax.shift_right_logical(code, 6)).astype(F32)
    low = (code & 63).astype(F32)
    hits = [jnp.where(owner == o, 1.0, 0.0).astype(F32) for o in range(owners)]
    before = jnp.where(iota((lanes, lanes), 0) < iota((lanes, lanes), 1), 1.0, 0.0).astype(BF)
    prefix = dot(jnp.concatenate(hits, axis=0).astype(BF), before)
    rank = jnp.zeros(ids.shape, F32)
    for o in range(owners):
        rank = rank + hits[o] * prefix[o * users : (o + 1) * users]
    rank = rank.astype(jnp.int32)
    total = jnp.zeros((2 * owners, 128), F32)
    for b in range(users):
        hit = iota((owners, lanes), 0) == owner[b : b + 1]
        left = jnp.concatenate(
            [jnp.where(hit, high[b : b + 1], 0.0), jnp.where(hit, low[b : b + 1], 0.0)], axis=0
        ).astype(BF)
        right = jnp.where(iota((128, lanes), 0) == rank[b : b + 1] + PER * b, 1.0, 0.0).astype(BF)
        total = total + dot(left, right, NT)
    codes = (total[:owners] * 64.0 + total[owners:]).astype(jnp.int32)
    slots = owner * 16 + rank
    for b in range(users):
        part = pl.ds(b * owners, owners)
        out[part, 0, :128] = codes
        out[part, 0, 128:] = jnp.broadcast_to(slots[b : b + 1], (owners, lanes))
    put = pltpu.make_async_copy(out, out_hbm, sems.at[2])
    put.start()
    put.wait()


def leaving_ids(order, ids, owners):
    hashes, users, length = ids.shape
    hbm = pl.BlockSpec(memory_space=pltpu.HBM)
    free = pl.BlockSpec(memory_space=pl.ANY)
    shape = (users * owners, 1, 384)
    return pl.pallas_call(
        ids_kernel,
        out_shape=jax.ShapeDtypeStruct(shape, jnp.int32),
        in_specs=[hbm, hbm],
        out_specs=free,
        scratch_shapes=[
            pltpu.SMEM((users,), jnp.int32),
            pltpu.VMEM(ids.shape, jnp.int32),
            pltpu.VMEM((users, 256), jnp.int32),
            pltpu.VMEM(shape, jnp.int32),
            pltpu.SemaphoreType.DMA((3,)),
        ],
        compiler_params=pltpu.CompilerParams(vmem_limit_bytes=60 * MIB),
        name="leaving_ids",
    )(order, ids)


def serve_kernel(got_hbm, table_hbm, first_out, second_hbm, codes, raw, wide, stages, second, sems):
    outs = (first_out, second)
    hashes, rows, width = table_hbm.shape
    tiles = width // 128
    requesters, half, _ = second.shape
    half_users = half // PER
    parts = 2 * hashes
    size = rows // 2
    get_codes = pltpu.make_async_copy(got_hbm.at[:, 0, pl.ds(0, 128)], codes, sems.at[parts])
    places = [(i // 2, (i % 2) * size) for i in range(parts)]
    copies = [
        pltpu.make_async_copy(
            table_hbm.at[h, pl.ds(first, size)], raw.at[h, pl.ds(first, size)], sems.at[i]
        )
        for i, (h, first) in enumerate(places)
    ]
    copies[0].start()
    get_codes.start()
    for copy in copies[1:]:
        copy.start()
    for i, (h, first) in enumerate(places):
        copies[i].wait()

        @pl.loop(0, size // 64)
        def _(g):
            for q in range(4):
                at = pl.multiple_of(first + g * 64 + q * 16, 16)
                for c in range(tiles):
                    both = raw[h, pl.ds(at, 16), c * 128 : (c + 1) * 128].astype(F32)
                    base = (h * rows + at) * tiles + c
                    wide[pl.ds(base, 8, stride=tiles), :] = both[:8]
                    wide[pl.ds(base + 8 * tiles, 8, stride=tiles), :] = both[8:]

    get_codes.wait()
    first_lane = lax.axis_index("batch") * PER

    def gather(side, t, part):
        for j in range(half_users):
            home = (part * half_users + j) * requesters + t
            for k in range(PER):
                row = codes[home, first_lane + k]
                slot = (j * PER + k) * tiles
                stages[side, slot : slot + tiles, :] = wide[
                    pl.ds(pl.multiple_of(row * tiles, tiles), tiles), :
                ]

    def pack(side, t, part):
        for g in range(half // 16):
            for c in range(tiles):
                base = g * 16 * tiles + c
                upper = stages[side, pl.ds(base, 8, stride=tiles), :]
                lower = stages[side, pl.ds(base + 8 * tiles, 8, stride=tiles), :]
                outs[part][t, g * 16 : (g + 1) * 16, c * 128 : (c + 1) * 128] = jnp.concatenate(
                    [upper, lower], axis=0
                ).astype(BF)

    gather(0, 0, 0)

    @pl.loop(0, requesters)
    def _(t):
        gather(1, t, 1)
        pack(0, t, 0)

        @pl.when(t + 1 < requesters)
        def _():
            gather(0, t + 1, 0)

        pack(1, t, 1)
        pltpu.make_async_copy(second.at[t], second_hbm.at[t], sems.at[parts + 1]).start()

    pltpu.make_async_copy(second, second_hbm, sems.at[parts + 1]).wait()


def serve_rows(got, tables, requesters, per_chunk):
    hashes, rows, width = tables.shape
    tiles = width // 128
    shape = (requesters, per_chunk, width)
    hbm = pl.BlockSpec(memory_space=pltpu.HBM)
    free = pl.BlockSpec(memory_space=pl.ANY)
    return pl.pallas_call(
        serve_kernel,
        out_shape=[jax.ShapeDtypeStruct(shape, BF)] * CHUNKS,
        in_specs=[free, hbm],
        out_specs=[pl.BlockSpec(memory_space=pltpu.VMEM), hbm],
        scratch_shapes=[
            pltpu.SMEM((got.shape[0], 128), jnp.int32),
            pltpu.VMEM(tables.shape, BF),
            pltpu.VMEM((hashes * rows * tiles, 128), F32),
            pltpu.VMEM((2, per_chunk * tiles, 128), F32),
            pltpu.VMEM(shape, BF),
            pltpu.SemaphoreType.DMA((2 * hashes + 2,)),
        ],
        compiler_params=pltpu.CompilerParams(vmem_limit_bytes=SERVE_VMEM),
        name="serve_rows",
    )(got, tables)


def sigmoid(z):
    return 0.5 + 0.5 * jnp.tanh(0.5 * z)


def layer_kernel(chunk, *refs):
    len_hbm, got_hbm, fetched, cot_hbm, w_in_hbm, w_out_hbm = refs[:6]
    enc_hbm, grad_hbm, *refs = refs[7:] if chunk else refs[6:]
    lengths, got, cot, enc, grads, w_in, w_out, x_s, n_s, gate_s, *refs = refs
    dsilu_s, qkv_s, mixed_s, s_s, w_s, dw_s, dz_s, mask_s, sems = refs
    users, length, width = cot.shape
    tokens = users * length
    head = width // HEADS
    owners, per_chunk, _ = fetched.shape
    halves = 1
    half_users = users // halves
    half_tokens = tokens // halves
    half_rows = per_chunk // halves
    half_slots = owners * half_rows
    pair = 2 * length
    mine = lax.axis_index("table")
    our_users = pl.ds(chunk * users, users)

    def fetch(i, src, dst):
        copy = pltpu.make_async_copy(src, dst, sems.at[i])
        copy.start()
        return copy

    get_len = fetch(0, len_hbm, lengths)
    get_slots = [
        fetch(1 + j, got_hbm.at[pl.ds((chunk * users + j) * owners + mine, 1)], got.at[pl.ds(j, 1)])
        for j in range(users)
    ]
    sem_at = 1 + users
    get_w = {
        c: fetch(
            sem_at + c, w_in_hbm.at[0, :, pl.ds(c * width, width)], w_in.at[:, pl.ds(c * width, width)]
        )
        for c in PARTS_ORDER
    }
    sem_at += 4
    get_w_out = fetch(sem_at, w_out_hbm.at[0], w_out)
    get_cot = fetch(sem_at + 1, cot_hbm.at[our_users], cot)
    sem_at += 2

    get_len.wait()
    for copy in get_slots:
        copy.wait()
    slot_rows, slot_cols = [], []
    for i in range(halves):
        rows_of = []
        for h in range(3):
            packed = jnp.concatenate(
                [
                    got[i * half_users + j, :, 128 + h * length : 128 + (h + 1) * length]
                    for j in range(half_users)
                ],
                axis=1,
            )
            rows_of.append(
                lax.shift_right_logical(packed, 4) * half_rows
                + lax.div(iota((1, half_tokens), 1), length) * PER
                + (packed & 15)
            )
        stacked = jnp.concatenate(rows_of + [jnp.zeros((5, half_tokens), jnp.int32)], axis=0)
        slot_rows.append(rows_of)
        slot_cols.append(stacked.astype(F32).T.astype(jnp.int32))
    picks = []
    for i in range(halves):
        lane = iota((half_tokens, half_slots), 1)
        pick = (lane == slot_cols[i][:, 0:1]) | (lane == slot_cols[i][:, 1:2])
        pick = pick | (lane == slot_cols[i][:, 2:3])
        picks.append(jnp.where(pick, 1.0, 0.0).astype(BF))

    token_user = lax.div(iota((tokens, 1), 0), length)
    token_pos = iota((tokens, 1), 0) - token_user * length
    token_len = jnp.zeros((tokens, 1), jnp.int32)
    for u in range(users):
        token_len = jnp.where(token_user == u, lengths[chunk * users + u], token_len)
    live = jnp.where(token_pos < token_len, 1.0, 0.0).astype(F32)
    key = iota((tokens, pair), 1)
    query = iota((tokens, pair), 0)
    same = lax.div(key, length) == lax.rem(lax.div(query, length), 2)
    causal = lax.rem(key, length) <= lax.rem(query, length)
    mask_s[...] = jnp.where(same & causal, 1.0, 0.0) * live

    for i in range(halves):
        rows = slice(i * half_tokens, (i + 1) * half_tokens)
        block = fetched[:, i * half_rows : (i + 1) * half_rows, :].reshape(half_slots, width)
        x_s[rows] = dot(picks[i], block).astype(BF).astype(F32)
    x = x_s[...]
    mean = jnp.mean(x, axis=1, keepdims=True)
    centered = x - mean
    rstd = lax.rsqrt(jnp.mean(centered * centered, axis=1, keepdims=True) + EPS)
    n_s[...] = (centered * rstd).astype(BF)

    step = STEP
    for c in PARTS_ORDER:
        get_w[c].wait()

        @pl.loop(0, width // step)
        def _(i, c=c):
            cols = pl.ds(pl.multiple_of(i * step, step), step)
            z = dot(n_s[...], w_in[:, pl.ds(pl.multiple_of(c * width + i * step, step), step)])
            sig = sigmoid(z)
            out = z * sig
            dsilu_s[c, :, cols] = sig + out * (1.0 - sig)
            if c == 0:
                gate_s[:, cols] = out
            else:
                qkv_s[c - 1, :, cols] = out.astype(BF)

    scale = head ** (-0.5)
    blocks = [
        (slice(p * pair, (p + 1) * pair), slice(h * head, (h + 1) * head))
        for h in range(HEADS)
        for p in range(tokens // pair)
    ]
    for at in blocks:
        s_s[at] = dot(qkv_s[(1, *at)], qkv_s[(2, *at)], NT)
    mask = mask_s[...]
    for h in range(HEADS):
        cols = slice(h * head, (h + 1) * head)
        s = s_s[:, cols] * scale
        sig = sigmoid(s)
        out = s * sig
        w_s[:, cols] = (out * mask).astype(BF)
        dw_s[:, cols] = (sig + out * (1.0 - sig)) * (mask * scale)
    for at in blocks:
        mixed_s[at] = dot(w_s[at], qkv_s[(0, *at)])

    mixed = mixed_s[...]
    mean2 = jnp.mean(mixed, axis=1, keepdims=True)
    centered2 = mixed - mean2
    rstd2 = lax.rsqrt(jnp.mean(centered2 * centered2, axis=1, keepdims=True) + EPS)
    hat = centered2 * rstd2
    gate = gate_s[...]
    gated = (hat * gate).astype(BF)
    get_w_out.wait()
    out = (x_s[...] + dot(gated, w_out[...])) * live
    enc[...] = out.astype(BF).reshape(users, length, width)
    send_enc = fetch(sem_at, enc, enc_hbm.at[our_users])
    sem_at += 1

    get_cot.wait()
    g = cot[...].reshape(tokens, width).astype(F32) * live
    dgated = dot(g.astype(BF), w_out[...], NT).astype(BF).astype(F32)
    dz_s[0] = (dgated * hat * dsilu_s[0]).astype(BF)
    dhat = dgated * gate
    dmixed = rstd2 * (
        dhat
        - jnp.mean(dhat, axis=1, keepdims=True)
        - hat * jnp.mean(dhat * hat, axis=1, keepdims=True)
    )
    n_s[...] = dmixed.astype(BF)
    for at in blocks:
        s_s[at] = dot(n_s[at], qkv_s[(0, *at)], NT)
    for at in blocks:
        dv = dot(w_s[at], n_s[at], TN).astype(BF).astype(F32)
        dz_s[(1, *at)] = (dv * dsilu_s[(1, *at)]).astype(BF)
    for h in range(HEADS):
        cols = slice(h * head, (h + 1) * head)
        w_s[:, cols] = (s_s[:, cols].astype(BF).astype(F32) * dw_s[:, cols]).astype(BF)
    for at in blocks:
        dq = dot(w_s[at], qkv_s[(2, *at)]).astype(BF).astype(F32)
        dz_s[(2, *at)] = (dq * dsilu_s[(2, *at)]).astype(BF)
    for at in blocks:
        dk = dot(w_s[at], qkv_s[(1, *at)], TN).astype(BF).astype(F32)
        dz_s[(3, *at)] = (dk * dsilu_s[(3, *at)]).astype(BF)

    @pl.loop(0, width // step)
    def _(i):
        cols = pl.ds(pl.multiple_of(i * step, step), step)
        dn = dot(dz_s[0], w_in[cols, :width], NT)
        for c in range(1, 4):
            dn = dn + dot(dz_s[c], w_in[cols, c * width : (c + 1) * width], NT)
        mixed_s[:, cols] = dn

    dn = mixed_s[...].astype(BF).astype(F32)
    xhat = (x_s[...] - mean) * rstd
    dx = rstd * (
        dn
        - jnp.mean(dn, axis=1, keepdims=True)
        - xhat * jnp.mean(dn * xhat, axis=1, keepdims=True)
    )
    n_s[...] = (dx + g).astype(BF)
    puts = []
    for i in range(halves):
        sub = iota((half_slots, half_tokens), 0)
        put = (sub == slot_rows[i][0]) | (sub == slot_rows[i][1]) | (sub == slot_rows[i][2])
        puts.append(jnp.where(put, 1.0, 0.0).astype(BF))
    ranks = grads.shape[0]
    copies = [send_enc]
    for b in range(0, ranks, 2):
        cols = slice(b * 128, (b + 2) * 128)
        for i in range(halves):
            rows = slice(i * half_tokens, (i + 1) * half_tokens)
            two = dot(puts[i], n_s[rows, cols]).astype(BF)
            for r in range(2):
                grads[b + r, :, i * half_rows : (i + 1) * half_rows, :] = two[
                    :, r * 128 : (r + 1) * 128
                ].reshape(owners, half_rows, 128)
        copies.append(fetch(sem_at, grads.at[pl.ds(b, 2)], grad_hbm.at[pl.ds(b, 2)]))
        sem_at += 1
    for copy in copies:
        copy.wait()


def layer(chunk, lengths, got, fetched, cot, w_in, w_out, batch_ranks, prev):
    owners, per_chunk, width = fetched.shape
    all_users, length, _ = cot.shape
    users = all_users // CHUNKS
    tokens = users * length
    ours = (users, length, width)
    grad_shape = (batch_ranks, owners, per_chunk, width // batch_ranks)
    hbm = pl.BlockSpec(memory_space=pltpu.HBM)
    free = pl.BlockSpec(memory_space=pl.ANY)
    vmem = pl.BlockSpec(memory_space=pltpu.VMEM)
    args = (lengths, got, fetched, cot, w_in, w_out) + ((prev,) if chunk else ())
    return pl.pallas_call(
        functools.partial(layer_kernel, chunk),
        out_shape=[
            jax.ShapeDtypeStruct(cot.shape, BF),
            jax.ShapeDtypeStruct(grad_shape, BF),
        ],
        in_specs=[hbm, free, vmem, hbm, hbm, hbm, hbm][: len(args)],
        out_specs=[hbm, hbm],
        input_output_aliases={6: 0} if chunk else {},
        scratch_shapes=[
            pltpu.SMEM((all_users,), jnp.int32),
            pltpu.VMEM((users, 1, got.shape[2]), jnp.int32),
            pltpu.VMEM(ours, BF),
            pltpu.VMEM(ours, BF),
            pltpu.VMEM(grad_shape, BF),
            pltpu.VMEM((width, 4 * width), BF),
            pltpu.VMEM((width, width), BF),
            pltpu.VMEM((tokens, width), F32),
            pltpu.VMEM((tokens, width), BF),
            pltpu.VMEM((tokens, width), F32),
            pltpu.VMEM((4, tokens, width), F32),
            pltpu.VMEM((3, tokens, width), BF),
            pltpu.VMEM((tokens, width), F32),
            pltpu.VMEM((tokens, width), F32),
            pltpu.VMEM((tokens, width), BF),
            pltpu.VMEM((tokens, width), F32),
            pltpu.VMEM((4, tokens, width), BF),
            pltpu.VMEM((tokens, 2 * length), F32),
            pltpu.SemaphoreType.DMA((10 + users + batch_ranks // 2,)),
        ],
        compiler_params=pltpu.CompilerParams(vmem_limit_bytes=LAYER_VMEM),
        cost_estimate=COST,
        name="layer",
    )(*args)


def arrange(chunk, got, codes, per_sender):
    group = codes.shape[1] // per_sender
    users = per_sender // PER
    lane = iota((OWNERS, 128), 1)
    for b in range(got.shape[0] // OWNERS):
        line = jnp.zeros((OWNERS, 128), jnp.int32)
        for j in range(users):
            home = (chunk * users + j) * OWNERS
            moved = pltpu.roll(got[home : home + OWNERS, 0, :], ((j - b) * PER) % 128, 1)
            line = jnp.where((lane >= j * PER) & (lane < (j + 1) * PER), moved, line)
        for t in range(OWNERS):
            sender = b * OWNERS + t
            first = (sender % group) * per_sender
            codes[sender // group : sender // group + 1, first : first + per_sender] = line[
                t : t + 1, :per_sender
            ]


def collect_kernel(chunk, given, rows, *refs):
    if chunk:
        prev_hbm, out_hbm, codes, wide, hits, out, prev, sems = refs
    else:
        out_hbm, next_hbm, got, codes, later, wide, hits, out, sems = refs
    senders, per_sender, cols = rows.shape
    groups, depth = codes.shape
    group = senders // groups
    parts = wide.shape[1] // cols
    height = out.shape[0] // parts
    if chunk:
        get_codes = pltpu.make_async_copy(given, codes, sems.at[0])
        get_prev = pltpu.make_async_copy(prev_hbm, prev, sems.at[1])
        get_codes.start()
        get_prev.start()
        get_codes.wait()
        get_prev.wait()
    else:
        get_ids = pltpu.make_async_copy(given.at[:, :, pl.ds(0, 128)], got, sems.at[0])
        get_ids.start()
        get_ids.wait()
        arrange(0, got, codes, per_sender)
    part_cols = lax.div(codes[...], height).astype(F32).T.astype(jnp.int32)
    for s in range(groups):
        inside = lax.rem(codes[s : s + 1, :], height)
        for q in range(height // 128):
            near = jnp.clip(inside - 128 * q, -1, 128).astype(F32).astype(BF)
            row = iota((128, depth), 0).astype(F32).astype(BF)
            hits[q * 128 : (q + 1) * 128, s * depth : (s + 1) * depth] = jnp.where(
                row == near, jnp.ones((), BF), jnp.zeros((), BF)
            )
        block = rows[s * group : (s + 1) * group].reshape(depth, cols)
        for p in range(parts):
            here = part_cols[:, s : s + 1] == p
            wide[s * depth : (s + 1) * depth, p * cols : (p + 1) * cols] = jnp.where(
                here, block, jnp.zeros_like(block)
            )
    acc = dot(hits[...], wide[...])
    puts = []
    for p in range(parts):
        at = slice(p * height, (p + 1) * height)
        part = acc[:, p * cols : (p + 1) * cols]
        out[at, :] = part + prev[at, :] if chunk else part
        puts.append(pltpu.make_async_copy(out.at[at], out_hbm.at[at], sems.at[2 + p]))
        puts[-1].start()
    if not chunk:
        arrange(1, got, later, per_sender)
        puts.append(pltpu.make_async_copy(later, next_hbm, sems.at[1]))
        puts[-1].start()
    for put in puts:
        put.wait()


def collect(chunk, given, rows, prev, total):
    senders, per_sender, cols = rows.shape
    hbm = pl.BlockSpec(memory_space=pltpu.HBM)
    free = pl.BlockSpec(memory_space=pl.ANY)
    vmem = pl.BlockSpec(memory_space=pltpu.VMEM)
    code_shape = (senders // GROUP, GROUP * per_sender)
    result = jax.ShapeDtypeStruct((total, cols), F32)
    ordered = pltpu.VMEM(code_shape, jnp.int32)
    before = [] if chunk else [pltpu.VMEM((given.shape[0], 1, 128), jnp.int32)]
    return pl.pallas_call(
        functools.partial(collect_kernel, chunk),
        out_shape=result if chunk else [result, jax.ShapeDtypeStruct(code_shape, jnp.int32)],
        in_specs=[free, vmem, hbm] if chunk else [free, vmem],
        out_specs=hbm if chunk else [hbm, hbm],
        scratch_shapes=before
        + [ordered] * (1 if chunk else 2)
        + [
            pltpu.VMEM((senders * per_sender, PARTS * cols), BF),
            pltpu.VMEM((total // PARTS, senders * per_sender), BF),
            pltpu.VMEM((total, cols), F32),
        ]
        + ([pltpu.VMEM((total, cols), F32)] if chunk else [])
        + [pltpu.SemaphoreType.DMA((2 + PARTS,))],
        compiler_params=pltpu.CompilerParams(vmem_limit_bytes=COLLECT_VMEM),
        cost_estimate=COST,
        name="collect",
    )(*((given, rows, prev) if chunk else (given, rows)))


def body(item_rows, send_order, user_lengths, tables, w_in, w_out, out_grad):
    batch_ranks = lax.axis_size("batch")
    table_ranks = lax.axis_size("table")
    users, length, hashes = item_rows.shape
    rows_local = tables.shape[1]
    both = ("batch", "table")
    per_chunk = users // CHUNKS * PER

    leaving = leaving_ids(send_order, item_rows.transpose(2, 0, 1), table_ranks)
    got = lax.all_to_all(leaving, both, 0, 0, tiled=True)
    served = serve_rows(got, tables, table_ranks, per_chunk)
    encoded, returned = None, []
    for c in range(CHUNKS):
        fetched = lax.all_to_all(served[c], "table", 0, 0, tiled=True)
        encoded, grads = layer(
            c, user_lengths, got, fetched, out_grad, w_in, w_out, batch_ranks, encoded
        )
        grads = grads.reshape(batch_ranks * table_ranks, per_chunk, -1)
        returned.append(lax.all_to_all(grads, both, 0, 0, tiled=True))
    total, codes = collect(0, got, returned[0], None, hashes * rows_local)
    total = collect(1, codes, returned[1], total, hashes * rows_local)
    return encoded, total.reshape(hashes, rows_local, -1)


def solution(mesh):
    in_specs = (
        P(("batch", "table"), None, None),
        P(("batch", "table")),
        P(("batch", "table")),
        P(None, "table", None),
        P(),
        P(),
        P(("batch", "table"), None, None),
    )
    out_specs = (P(("batch", "table"), None, None), P(None, "table", "batch"))
    return jax.shard_map(body, mesh=mesh, in_specs=in_specs, out_specs=out_specs, check_vma=False)
```

```python
import functools

import jax
import jax.numpy as jnp
from jax import lax
from jax.experimental import pallas as pl
from jax.experimental.pallas import tpu as pltpu
from jax.sharding import PartitionSpec as P

HEADS = 8
PER = 12
EPS = 1e-05
BF = jnp.bfloat16
F32 = jnp.float32
NT = (((1,), (1,)), ((), ()))
NN = (((1,), (0,)), ((), ()))
TN = (((0,), (0,)), ((), ()))
CHUNKS = 2
MIB = 1024 * 1024
LAYER_VMEM = 49 * MIB
SERVE_VMEM = 50 * MIB
COLLECT_VMEM = 52 * MIB
PARTS = 4
OWNERS = 16
GROUP = 16
COST = pl.CostEstimate(flops=12_000_000_000, bytes_accessed=20_000_000, transcendentals=0)
PARTS_ORDER = (2, 3, 1, 0)
STEP = 256


def dot(a, b, dims=NN):
    return lax.dot_general(a, b, dims, preferred_element_type=F32)


def iota(shape, dim):
    return lax.broadcasted_iota(jnp.int32, shape, dim)


def ids_kernel(order_hbm, ids_hbm, out_hbm, order, raw, ids_scr, out, sems):
    hashes, users, length = raw.shape
    owners = out.shape[0] // users
    get_order = pltpu.make_async_copy(order_hbm, order, sems.at[0])
    get_ids = pltpu.make_async_copy(ids_hbm, raw, sems.at[1])
    get_order.start()
    get_ids.start()
    ids_scr[...] = jnp.full(ids_scr.shape, -1, jnp.int32)
    get_order.wait()
    get_ids.wait()
    for b in range(users):
        user = order[b]
        for h in range(hashes):
            ids_scr[b : b + 1, h * length : (h + 1) * length] = raw[h, pl.ds(user, 1), :]
    ids = ids_scr[...]
    lanes = ids.shape[1]
    owner = lax.shift_right_arithmetic(ids, 10)
    hash_of = lax.div(iota(ids.shape, 1), length)
    code = (ids & 1023) + 1024 * hash_of
    high = (lax.shift_right_logical(code, 6)).astype(F32)
    low = (code & 63).astype(F32)
    hits = [jnp.where(owner == o, 1.0, 0.0).astype(F32) for o in range(owners)]
    before = jnp.where(iota((lanes, lanes), 0) < iota((lanes, lanes), 1), 1.0, 0.0).astype(BF)
    prefix = dot(jnp.concatenate(hits, axis=0).astype(BF), before)
    rank = jnp.zeros(ids.shape, F32)
    for o in range(owners):
        rank = rank + hits[o] * prefix[o * users : (o + 1) * users]
    rank = rank.astype(jnp.int32)
    total = jnp.zeros((2 * owners, 128), F32)
    for b in range(users):
        hit = iota((owners, lanes), 0) == owner[b : b + 1]
        left = jnp.concatenate(
            [jnp.where(hit, high[b : b + 1], 0.0), jnp.where(hit, low[b : b + 1], 0.0)], axis=0
        ).astype(BF)
        right = jnp.where(iota((128, lanes), 0) == rank[b : b + 1] + PER * b, 1.0, 0.0).astype(BF)
        total = total + dot(left, right, NT)
    codes = (total[:owners] * 64.0 + total[owners:]).astype(jnp.int32)
    slots = owner * 16 + rank
    for b in range(users):
        part = pl.ds(b * owners, owners)
        out[part, 0, :128] = codes
        out[part, 0, 128:] = jnp.broadcast_to(slots[b : b + 1], (owners, lanes))
    put = pltpu.make_async_copy(out, out_hbm, sems.at[2])
    put.start()
    put.wait()


def leaving_ids(order, ids, owners):
    hashes, users, length = ids.shape
    hbm = pl.BlockSpec(memory_space=pltpu.HBM)
    free = pl.BlockSpec(memory_space=pl.ANY)
    shape = (users * owners, 1, 384)
    return pl.pallas_call(
        ids_kernel,
        out_shape=jax.ShapeDtypeStruct(shape, jnp.int32),
        in_specs=[hbm, hbm],
        out_specs=free,
        scratch_shapes=[
            pltpu.SMEM((users,), jnp.int32),
            pltpu.VMEM(ids.shape, jnp.int32),
            pltpu.VMEM((users, 256), jnp.int32),
            pltpu.VMEM(shape, jnp.int32),
            pltpu.SemaphoreType.DMA((3,)),
        ],
        compiler_params=pltpu.CompilerParams(vmem_limit_bytes=60 * MIB),
        name="leaving_ids",
    )(order, ids)


def serve_kernel(got_hbm, table_hbm, first_out, second_hbm, codes, raw, wide, stages, second, sems):
    outs = (first_out, second)
    hashes, rows, width = table_hbm.shape
    tiles = width // 128
    requesters, half, _ = second.shape
    half_users = half // PER
    parts = 2 * hashes
    size = rows // 2
    get_codes = pltpu.make_async_copy(got_hbm.at[:, 0, pl.ds(0, 128)], codes, sems.at[parts])
    places = [(i // 2, (i % 2) * size) for i in range(parts)]
    copies = [
        pltpu.make_async_copy(
            table_hbm.at[h, pl.ds(first, size)], raw.at[h, pl.ds(first, size)], sems.at[i]
        )
        for i, (h, first) in enumerate(places)
    ]
    copies[0].start()
    get_codes.start()
    for copy in copies[1:]:
        copy.start()
    for i, (h, first) in enumerate(places):
        copies[i].wait()

        @pl.loop(0, size // 64)
        def _(g):
            for q in range(4):
                at = pl.multiple_of(first + g * 64 + q * 16, 16)
                for c in range(tiles):
                    both = raw[h, pl.ds(at, 16), c * 128 : (c + 1) * 128].astype(F32)
                    base = (h * rows + at) * tiles + c
                    wide[pl.ds(base, 8, stride=tiles), :] = both[:8]
                    wide[pl.ds(base + 8 * tiles, 8, stride=tiles), :] = both[8:]

    get_codes.wait()
    first_lane = lax.axis_index("batch") * PER

    def gather(side, t, part):
        for j in range(half_users):
            home = (part * half_users + j) * requesters + t
            for k in range(PER):
                row = codes[home, first_lane + k]
                slot = (j * PER + k) * tiles
                stages[side, slot : slot + tiles, :] = wide[
                    pl.ds(pl.multiple_of(row * tiles, tiles), tiles), :
                ]

    def pack(side, t, part):
        for g in range(half // 16):
            for c in range(tiles):
                base = g * 16 * tiles + c
                upper = stages[side, pl.ds(base, 8, stride=tiles), :]
                lower = stages[side, pl.ds(base + 8 * tiles, 8, stride=tiles), :]
                outs[part][t, g * 16 : (g + 1) * 16, c * 128 : (c + 1) * 128] = jnp.concatenate(
                    [upper, lower], axis=0
                ).astype(BF)

    gather(0, 0, 0)

    @pl.loop(0, requesters)
    def _(t):
        gather(1, t, 1)
        pack(0, t, 0)

        @pl.when(t + 1 < requesters)
        def _():
            gather(0, t + 1, 0)

        pack(1, t, 1)
        pltpu.make_async_copy(second.at[t], second_hbm.at[t], sems.at[parts + 1]).start()

    pltpu.make_async_copy(second, second_hbm, sems.at[parts + 1]).wait()


def serve_rows(got, tables, requesters, per_chunk):
    hashes, rows, width = tables.shape
    tiles = width // 128
    shape = (requesters, per_chunk, width)
    hbm = pl.BlockSpec(memory_space=pltpu.HBM)
    free = pl.BlockSpec(memory_space=pl.ANY)
    return pl.pallas_call(
        serve_kernel,
        out_shape=[jax.ShapeDtypeStruct(shape, BF)] * CHUNKS,
        in_specs=[free, hbm],
        out_specs=[pl.BlockSpec(memory_space=pltpu.VMEM), hbm],
        scratch_shapes=[
            pltpu.SMEM((got.shape[0], 128), jnp.int32),
            pltpu.VMEM(tables.shape, BF),
            pltpu.VMEM((hashes * rows * tiles, 128), F32),
            pltpu.VMEM((2, per_chunk * tiles, 128), F32),
            pltpu.VMEM(shape, BF),
            pltpu.SemaphoreType.DMA((2 * hashes + 2,)),
        ],
        compiler_params=pltpu.CompilerParams(vmem_limit_bytes=SERVE_VMEM),
        name="serve_rows",
    )(got, tables)


def sigmoid(z):
    return 0.5 + 0.5 * jnp.tanh(0.5 * z)


def layer_kernel(chunk, *refs):
    len_hbm, got_hbm, fetched, cot_hbm, w_in_hbm, w_out_hbm = refs[:6]
    enc_hbm, grad_hbm, *refs = refs[7:] if chunk else refs[6:]
    lengths, got, cot, enc, grads, w_in, w_out, x_s, n_s, gate_s, *refs = refs
    dsilu_s, qkv_s, mixed_s, s_s, w_s, dw_s, dz_s, mask_s, sems = refs
    users, length, width = cot.shape
    tokens = users * length
    head = width // HEADS
    owners, per_chunk, _ = fetched.shape
    halves = 1
    half_users = users // halves
    half_tokens = tokens // halves
    half_rows = per_chunk // halves
    half_slots = owners * half_rows
    pair = 2 * length
    mine = lax.axis_index("table")
    our_users = pl.ds(chunk * users, users)

    def fetch(i, src, dst):
        copy = pltpu.make_async_copy(src, dst, sems.at[i])
        copy.start()
        return copy

    get_len = fetch(0, len_hbm, lengths)
    get_slots = [
        fetch(1 + j, got_hbm.at[pl.ds((chunk * users + j) * owners + mine, 1)], got.at[pl.ds(j, 1)])
        for j in range(users)
    ]
    sem_at = 1 + users
    get_w = {
        c: fetch(
            sem_at + c, w_in_hbm.at[0, :, pl.ds(c * width, width)], w_in.at[:, pl.ds(c * width, width)]
        )
        for c in PARTS_ORDER
    }
    sem_at += 4
    get_w_out = fetch(sem_at, w_out_hbm.at[0], w_out)
    get_cot = fetch(sem_at + 1, cot_hbm.at[our_users], cot)
    sem_at += 2

    get_len.wait()
    for copy in get_slots:
        copy.wait()
    slot_rows, slot_cols = [], []
    for i in range(halves):
        rows_of = []
        for h in range(3):
            packed = jnp.concatenate(
                [
                    got[i * half_users + j, :, 128 + h * length : 128 + (h + 1) * length]
                    for j in range(half_users)
                ],
                axis=1,
            )
            rows_of.append(
                lax.shift_right_logical(packed, 4) * half_rows
                + lax.div(iota((1, half_tokens), 1), length) * PER
                + (packed & 15)
            )
        stacked = jnp.concatenate(rows_of + [jnp.zeros((5, half_tokens), jnp.int32)], axis=0)
        slot_rows.append(rows_of)
        slot_cols.append(stacked.astype(F32).T.astype(jnp.int32))
    picks = []
    for i in range(halves):
        lane = iota((half_tokens, half_slots), 1)
        pick = (lane == slot_cols[i][:, 0:1]) | (lane == slot_cols[i][:, 1:2])
        pick = pick | (lane == slot_cols[i][:, 2:3])
        picks.append(jnp.where(pick, 1.0, 0.0).astype(BF))

    token_user = lax.div(iota((tokens, 1), 0), length)
    token_pos = iota((tokens, 1), 0) - token_user * length
    token_len = jnp.zeros((tokens, 1), jnp.int32)
    for u in range(users):
        token_len = jnp.where(token_user == u, lengths[chunk * users + u], token_len)
    live = jnp.where(token_pos < token_len, 1.0, 0.0).astype(F32)
    key = iota((tokens, pair), 1)
    query = iota((tokens, pair), 0)
    same = lax.div(key, length) == lax.rem(lax.div(query, length), 2)
    causal = lax.rem(key, length) <= lax.rem(query, length)
    mask_s[...] = jnp.where(same & causal, 1.0, 0.0) * live

    for i in range(halves):
        rows = slice(i * half_tokens, (i + 1) * half_tokens)
        block = fetched[:, i * half_rows : (i + 1) * half_rows, :].reshape(half_slots, width)
        x_s[rows] = dot(picks[i], block).astype(BF).astype(F32)
    x = x_s[...]
    mean = jnp.mean(x, axis=1, keepdims=True)
    centered = x - mean
    rstd = lax.rsqrt(jnp.mean(centered * centered, axis=1, keepdims=True) + EPS)
    n_s[...] = (centered * rstd).astype(BF)

    step = STEP
    for c in PARTS_ORDER:
        get_w[c].wait()

        @pl.loop(0, width // step)
        def _(i, c=c):
            cols = pl.ds(pl.multiple_of(i * step, step), step)
            z = dot(n_s[...], w_in[:, pl.ds(pl.multiple_of(c * width + i * step, step), step)])
            sig = sigmoid(z)
            out = z * sig
            dsilu_s[c, :, cols] = sig + out * (1.0 - sig)
            if c == 0:
                gate_s[:, cols] = out
            else:
                qkv_s[c - 1, :, cols] = out.astype(BF)

    scale = head ** (-0.5)
    blocks = [
        (slice(p * pair, (p + 1) * pair), slice(h * head, (h + 1) * head))
        for h in range(HEADS)
        for p in range(tokens // pair)
    ]
    for at in blocks:
        s_s[at] = dot(qkv_s[(1, *at)], qkv_s[(2, *at)], NT)
    mask = mask_s[...]
    for h in range(HEADS):
        cols = slice(h * head, (h + 1) * head)
        s = s_s[:, cols] * scale
        sig = sigmoid(s)
        out = s * sig
        w_s[:, cols] = (out * mask).astype(BF)
        dw_s[:, cols] = (sig + out * (1.0 - sig)) * (mask * scale)
    for at in blocks:
        mixed_s[at] = dot(w_s[at], qkv_s[(0, *at)])

    mixed = mixed_s[...]
    mean2 = jnp.mean(mixed, axis=1, keepdims=True)
    centered2 = mixed - mean2
    rstd2 = lax.rsqrt(jnp.mean(centered2 * centered2, axis=1, keepdims=True) + EPS)
    hat = centered2 * rstd2
    gate = gate_s[...]
    gated = (hat * gate).astype(BF)
    get_w_out.wait()
    out = (x_s[...] + dot(gated, w_out[...])) * live
    enc[...] = out.astype(BF).reshape(users, length, width)
    send_enc = fetch(sem_at, enc, enc_hbm.at[our_users])
    sem_at += 1

    get_cot.wait()
    g = cot[...].reshape(tokens, width).astype(F32) * live
    dgated = dot(g.astype(BF), w_out[...], NT).astype(BF).astype(F32)
    dz_s[0] = (dgated * hat * dsilu_s[0]).astype(BF)
    dhat = dgated * gate
    dmixed = rstd2 * (
        dhat
        - jnp.mean(dhat, axis=1, keepdims=True)
        - hat * jnp.mean(dhat * hat, axis=1, keepdims=True)
    )
    n_s[...] = dmixed.astype(BF)
    for at in blocks:
        s_s[at] = dot(n_s[at], qkv_s[(0, *at)], NT)
    for at in blocks:
        dv = dot(w_s[at], n_s[at], TN).astype(BF).astype(F32)
        dz_s[(1, *at)] = (dv * dsilu_s[(1, *at)]).astype(BF)
    for h in range(HEADS):
        cols = slice(h * head, (h + 1) * head)
        w_s[:, cols] = (s_s[:, cols].astype(BF).astype(F32) * dw_s[:, cols]).astype(BF)
    for at in blocks:
        dq = dot(w_s[at], qkv_s[(2, *at)]).astype(BF).astype(F32)
        dz_s[(2, *at)] = (dq * dsilu_s[(2, *at)]).astype(BF)
    for at in blocks:
        dk = dot(w_s[at], qkv_s[(1, *at)], TN).astype(BF).astype(F32)
        dz_s[(3, *at)] = (dk * dsilu_s[(3, *at)]).astype(BF)

    @pl.loop(0, width // step)
    def _(i):
        cols = pl.ds(pl.multiple_of(i * step, step), step)
        dn = dot(dz_s[0], w_in[cols, :width], NT)
        for c in range(1, 4):
            dn = dn + dot(dz_s[c], w_in[cols, c * width : (c + 1) * width], NT)
        mixed_s[:, cols] = dn

    dn = mixed_s[...].astype(BF).astype(F32)
    xhat = (x_s[...] - mean) * rstd
    dx = rstd * (
        dn
        - jnp.mean(dn, axis=1, keepdims=True)
        - xhat * jnp.mean(dn * xhat, axis=1, keepdims=True)
    )
    n_s[...] = (dx + g).astype(BF)
    puts = []
    for i in range(halves):
        sub = iota((half_slots, half_tokens), 0)
        put = (sub == slot_rows[i][0]) | (sub == slot_rows[i][1]) | (sub == slot_rows[i][2])
        puts.append(jnp.where(put, 1.0, 0.0).astype(BF))
    ranks = grads.shape[0]
    copies = [send_enc]
    for b in range(0, ranks, 2):
        cols = slice(b * 128, (b + 2) * 128)
        for i in range(halves):
            rows = slice(i * half_tokens, (i + 1) * half_tokens)
            two = dot(puts[i], n_s[rows, cols]).astype(BF)
            for r in range(2):
                grads[b + r, :, i * half_rows : (i + 1) * half_rows, :] = two[
                    :, r * 128 : (r + 1) * 128
                ].reshape(owners, half_rows, 128)
        copies.append(fetch(sem_at, grads.at[pl.ds(b, 2)], grad_hbm.at[pl.ds(b, 2)]))
        sem_at += 1
    for copy in copies:
        copy.wait()


def layer(chunk, lengths, got, fetched, cot, w_in, w_out, batch_ranks, prev):
    owners, per_chunk, width = fetched.shape
    all_users, length, _ = cot.shape
    users = all_users // CHUNKS
    tokens = users * length
    ours = (users, length, width)
    grad_shape = (batch_ranks, owners, per_chunk, width // batch_ranks)
    hbm = pl.BlockSpec(memory_space=pltpu.HBM)
    free = pl.BlockSpec(memory_space=pl.ANY)
    vmem = pl.BlockSpec(memory_space=pltpu.VMEM)
    args = (lengths, got, fetched, cot, w_in, w_out) + ((prev,) if chunk else ())
    return pl.pallas_call(
        functools.partial(layer_kernel, chunk),
        out_shape=[
            jax.ShapeDtypeStruct(cot.shape, BF),
            jax.ShapeDtypeStruct(grad_shape, BF),
        ],
        in_specs=[hbm, free, vmem, hbm, hbm, hbm, hbm][: len(args)],
        out_specs=[hbm, hbm],
        input_output_aliases={6: 0} if chunk else {},
        scratch_shapes=[
            pltpu.SMEM((all_users,), jnp.int32),
            pltpu.VMEM((users, 1, got.shape[2]), jnp.int32),
            pltpu.VMEM(ours, BF),
            pltpu.VMEM(ours, BF),
            pltpu.VMEM(grad_shape, BF),
            pltpu.VMEM((width, 4 * width), BF),
            pltpu.VMEM((width, width), BF),
            pltpu.VMEM((tokens, width), F32),
            pltpu.VMEM((tokens, width), BF),
            pltpu.VMEM((tokens, width), F32),
            pltpu.VMEM((4, tokens, width), F32),
            pltpu.VMEM((3, tokens, width), BF),
            pltpu.VMEM((tokens, width), F32),
            pltpu.VMEM((tokens, width), F32),
            pltpu.VMEM((tokens, width), BF),
            pltpu.VMEM((tokens, width), F32),
            pltpu.VMEM((4, tokens, width), BF),
            pltpu.VMEM((tokens, 2 * length), F32),
            pltpu.SemaphoreType.DMA((10 + users + batch_ranks // 2,)),
        ],
        compiler_params=pltpu.CompilerParams(vmem_limit_bytes=LAYER_VMEM),
        cost_estimate=COST,
        name="layer",
    )(*args)


def arrange(chunk, got, codes, per_sender):
    group = codes.shape[1] // per_sender
    users = per_sender // PER
    lane = iota((OWNERS, 128), 1)
    for b in range(got.shape[0] // OWNERS):
        line = jnp.zeros((OWNERS, 128), jnp.int32)
        for j in range(users):
            home = (chunk * users + j) * OWNERS
            moved = pltpu.roll(got[home : home + OWNERS, 0, :], ((j - b) * PER) % 128, 1)
            line = jnp.where((lane >= j * PER) & (lane < (j + 1) * PER), moved, line)
        for t in range(OWNERS):
            sender = b * OWNERS + t
            first = (sender % group) * per_sender
            codes[sender // group : sender // group + 1, first : first + per_sender] = line[
                t : t + 1, :per_sender
            ]


def collect_kernel(chunk, given, rows, *refs):
    if chunk:
        prev_hbm, out_hbm, codes, wide, hits, out, prev, sems = refs
    else:
        out_hbm, next_hbm, got, codes, later, wide, hits, out, sems = refs
    senders, per_sender, cols = rows.shape
    groups, depth = codes.shape
    group = senders // groups
    parts = wide.shape[1] // cols
    height = out.shape[0] // parts
    if chunk:
        get_codes = pltpu.make_async_copy(given, codes, sems.at[0])
        get_prev = pltpu.make_async_copy(prev_hbm, prev, sems.at[1])
        get_codes.start()
        get_prev.start()
        get_codes.wait()
    else:
        get_ids = pltpu.make_async_copy(given.at[:, :, pl.ds(0, 128)], got, sems.at[0])
        get_ids.start()
        get_ids.wait()
        arrange(0, got, codes, per_sender)
    part_cols = lax.div(codes[...], height).astype(F32).T.astype(jnp.int32)
    for s in range(groups):
        inside = lax.rem(codes[s : s + 1, :], height)
        for q in range(height // 128):
            near = jnp.clip(inside - 128 * q, -1, 128).astype(F32).astype(BF)
            row = iota((128, depth), 0).astype(F32).astype(BF)
            hits[q * 128 : (q + 1) * 128, s * depth : (s + 1) * depth] = jnp.where(
                row == near, jnp.ones((), BF), jnp.zeros((), BF)
            )
        block = rows[s * group : (s + 1) * group].reshape(depth, cols)
        for p in range(parts):
            here = part_cols[:, s : s + 1] == p
            wide[s * depth : (s + 1) * depth, p * cols : (p + 1) * cols] = jnp.where(
                here, block, jnp.zeros_like(block)
            )
    acc = dot(hits[...], wide[...])
    if chunk:
        get_prev.wait()
    puts = []
    for p in range(parts):
        at = slice(p * height, (p + 1) * height)
        part = acc[:, p * cols : (p + 1) * cols]
        out[at, :] = part + prev[at, :] if chunk else part
        puts.append(pltpu.make_async_copy(out.at[at], out_hbm.at[at], sems.at[2 + p]))
        puts[-1].start()
    if not chunk:
        arrange(1, got, later, per_sender)
        puts.append(pltpu.make_async_copy(later, next_hbm, sems.at[1]))
        puts[-1].start()
    for put in puts:
        put.wait()


def collect(chunk, given, rows, prev, total):
    senders, per_sender, cols = rows.shape
    hbm = pl.BlockSpec(memory_space=pltpu.HBM)
    free = pl.BlockSpec(memory_space=pl.ANY)
    vmem = pl.BlockSpec(memory_space=pltpu.VMEM)
    code_shape = (senders // GROUP, GROUP * per_sender)
    result = jax.ShapeDtypeStruct((total, cols), F32)
    ordered = pltpu.VMEM(code_shape, jnp.int32)
    before = [] if chunk else [pltpu.VMEM((given.shape[0], 1, 128), jnp.int32)]
    return pl.pallas_call(
        functools.partial(collect_kernel, chunk),
        out_shape=result if chunk else [result, jax.ShapeDtypeStruct(code_shape, jnp.int32)],
        in_specs=[free, vmem, hbm] if chunk else [free, vmem],
        out_specs=hbm if chunk else [hbm, hbm],
        scratch_shapes=before
        + [ordered] * (1 if chunk else 2)
        + [
            pltpu.VMEM((senders * per_sender, PARTS * cols), BF),
            pltpu.VMEM((total // PARTS, senders * per_sender), BF),
            pltpu.VMEM((total, cols), F32),
        ]
        + ([pltpu.VMEM((total, cols), F32)] if chunk else [])
        + [pltpu.SemaphoreType.DMA((2 + PARTS,))],
        compiler_params=pltpu.CompilerParams(vmem_limit_bytes=COLLECT_VMEM),
        cost_estimate=COST,
        name="collect",
    )(*((given, rows, prev) if chunk else (given, rows)))


def body(item_rows, send_order, user_lengths, tables, w_in, w_out, out_grad):
    batch_ranks = lax.axis_size("batch")
    table_ranks = lax.axis_size("table")
    users, length, hashes = item_rows.shape
    rows_local = tables.shape[1]
    both = ("batch", "table")
    per_chunk = users // CHUNKS * PER

    leaving = leaving_ids(send_order, item_rows.transpose(2, 0, 1), table_ranks)
    got = lax.all_to_all(leaving, both, 0, 0, tiled=True)
    served = serve_rows(got, tables, table_ranks, per_chunk)
    encoded, returned = None, []
    for c in range(CHUNKS):
        fetched = lax.all_to_all(served[c], "table", 0, 0, tiled=True)
        encoded, grads = layer(
            c, user_lengths, got, fetched, out_grad, w_in, w_out, batch_ranks, encoded
        )
        grads = grads.reshape(batch_ranks * table_ranks, per_chunk, -1)
        returned.append(lax.all_to_all(grads, both, 0, 0, tiled=True))
    total, codes = collect(0, got, returned[0], None, hashes * rows_local)
    total = collect(1, codes, returned[1], total, hashes * rows_local)
    return encoded, total.reshape(hashes, rows_local, -1)


def solution(mesh):
    in_specs = (
        P(("batch", "table"), None, None),
        P(("batch", "table")),
        P(("batch", "table")),
        P(None, "table", None),
        P(),
        P(),
        P(("batch", "table"), None, None),
    )
    out_specs = (P(("batch", "table"), None, None), P(None, "table", "batch"))
    return jax.shard_map(body, mesh=mesh, in_specs=in_specs, out_specs=out_specs, check_vma=False)
```

```python
import functools

import jax
import jax.numpy as jnp
from jax import lax
from jax.experimental import pallas as pl
from jax.experimental.pallas import tpu as pltpu
from jax.sharding import PartitionSpec as P

HEADS = 8
PER = 12
EPS = 1e-05
BF = jnp.bfloat16
F32 = jnp.float32
NT = (((1,), (1,)), ((), ()))
NN = (((1,), (0,)), ((), ()))
TN = (((0,), (0,)), ((), ()))
CHUNKS = 2
MIB = 1024 * 1024
LAYER_VMEM = 49 * MIB
SERVE_VMEM = 50 * MIB
COLLECT_VMEM = 52 * MIB
PARTS = 4
OWNERS = 16
GROUP = 16
COST = pl.CostEstimate(flops=12_000_000_000, bytes_accessed=20_000_000, transcendentals=0)
PARTS_ORDER = (2, 3, 1, 0)
STEP = 256


def dot(a, b, dims=NN):
    return lax.dot_general(a, b, dims, preferred_element_type=F32)


def iota(shape, dim):
    return lax.broadcasted_iota(jnp.int32, shape, dim)


def ids_kernel(order_hbm, ids_hbm, out_hbm, order, raw, ids_scr, out, sems):
    hashes, users, length = raw.shape
    owners = out.shape[0] // users
    get_order = pltpu.make_async_copy(order_hbm, order, sems.at[0])
    get_ids = pltpu.make_async_copy(ids_hbm, raw, sems.at[1])
    get_order.start()
    get_ids.start()
    ids_scr[...] = jnp.full(ids_scr.shape, -1, jnp.int32)
    get_order.wait()
    get_ids.wait()
    for b in range(users):
        user = order[b]
        for h in range(hashes):
            ids_scr[b : b + 1, h * length : (h + 1) * length] = raw[h, pl.ds(user, 1), :]
    ids = ids_scr[...]
    lanes = ids.shape[1]
    owner = lax.shift_right_arithmetic(ids, 10)
    hash_of = lax.div(iota(ids.shape, 1), length)
    code = (ids & 1023) + 1024 * hash_of
    high = (lax.shift_right_logical(code, 6)).astype(F32)
    low = (code & 63).astype(F32)
    hits = [jnp.where(owner == o, 1.0, 0.0).astype(F32) for o in range(owners)]
    before = jnp.where(iota((lanes, lanes), 0) < iota((lanes, lanes), 1), 1.0, 0.0).astype(BF)
    prefix = dot(jnp.concatenate(hits, axis=0).astype(BF), before)
    rank = jnp.zeros(ids.shape, F32)
    for o in range(owners):
        rank = rank + hits[o] * prefix[o * users : (o + 1) * users]
    rank = rank.astype(jnp.int32)
    total = jnp.zeros((2 * owners, 128), F32)
    for b in range(users):
        hit = iota((owners, lanes), 0) == owner[b : b + 1]
        left = jnp.concatenate(
            [jnp.where(hit, high[b : b + 1], 0.0), jnp.where(hit, low[b : b + 1], 0.0)], axis=0
        ).astype(BF)
        right = jnp.where(iota((128, lanes), 0) == rank[b : b + 1] + PER * b, 1.0, 0.0).astype(BF)
        total = total + dot(left, right, NT)
    codes = (total[:owners] * 64.0 + total[owners:]).astype(jnp.int32)
    slots = owner * 16 + rank
    puts = []
    for b in range(users):
        part = pl.ds(b * owners, owners)
        out[part, 0, :128] = codes
        out[part, 0, 128:] = jnp.broadcast_to(slots[b : b + 1], (owners, lanes))
        puts.append(pltpu.make_async_copy(out.at[part], out_hbm.at[part], sems.at[2 + b]))
        puts[-1].start()
    for put in puts:
        put.wait()


def leaving_ids(order, ids, owners):
    hashes, users, length = ids.shape
    hbm = pl.BlockSpec(memory_space=pltpu.HBM)
    free = pl.BlockSpec(memory_space=pl.ANY)
    shape = (users * owners, 1, 384)
    return pl.pallas_call(
        ids_kernel,
        out_shape=jax.ShapeDtypeStruct(shape, jnp.int32),
        in_specs=[hbm, hbm],
        out_specs=free,
        scratch_shapes=[
            pltpu.SMEM((users,), jnp.int32),
            pltpu.VMEM(ids.shape, jnp.int32),
            pltpu.VMEM((users, 256), jnp.int32),
            pltpu.VMEM(shape, jnp.int32),
            pltpu.SemaphoreType.DMA((2 + users,)),
        ],
        compiler_params=pltpu.CompilerParams(vmem_limit_bytes=60 * MIB),
        name="leaving_ids",
    )(order, ids)


def serve_kernel(got_hbm, table_hbm, first_out, second_hbm, codes, raw, wide, stages, second, sems):
    outs = (first_out, second)
    hashes, rows, width = table_hbm.shape
    tiles = width // 128
    requesters, half, _ = second.shape
    half_users = half // PER
    parts = 2 * hashes
    size = rows // 2
    get_codes = pltpu.make_async_copy(got_hbm.at[:, 0, pl.ds(0, 128)], codes, sems.at[parts])
    places = [(i // 2, (i % 2) * size) for i in range(parts)]
    copies = [
        pltpu.make_async_copy(
            table_hbm.at[h, pl.ds(first, size)], raw.at[h, pl.ds(first, size)], sems.at[i]
        )
        for i, (h, first) in enumerate(places)
    ]
    copies[0].start()
    get_codes.start()
    for copy in copies[1:]:
        copy.start()
    for i, (h, first) in enumerate(places):
        copies[i].wait()

        @pl.loop(0, size // 64, unroll=2)
        def _(g):
            for q in range(4):
                at = pl.multiple_of(first + g * 64 + q * 16, 16)
                for c in range(tiles):
                    both = raw[h, pl.ds(at, 16), c * 128 : (c + 1) * 128].astype(F32)
                    base = (h * rows + at) * tiles + c
                    wide[pl.ds(base, 8, stride=tiles), :] = both[:8]
                    wide[pl.ds(base + 8 * tiles, 8, stride=tiles), :] = both[8:]

    get_codes.wait()
    first_lane = lax.axis_index("batch") * PER

    def gather(side, t, part):
        for j in range(half_users):
            home = (part * half_users + j) * requesters + t
            for k in range(PER):
                row = codes[home, first_lane + k]
                slot = (j * PER + k) * tiles
                stages[side, slot : slot + tiles, :] = wide[
                    pl.ds(pl.multiple_of(row * tiles, tiles), tiles), :
                ]

    def pack(side, t, part):
        for g in range(half // 16):
            for c in range(tiles):
                base = g * 16 * tiles + c
                upper = stages[side, pl.ds(base, 8, stride=tiles), :]
                lower = stages[side, pl.ds(base + 8 * tiles, 8, stride=tiles), :]
                outs[part][t, g * 16 : (g + 1) * 16, c * 128 : (c + 1) * 128] = jnp.concatenate(
                    [upper, lower], axis=0
                ).astype(BF)

    gather(0, 0, 0)

    @pl.loop(0, requesters)
    def _(t):
        gather(1, t, 1)
        pack(0, t, 0)

        @pl.when(t + 1 < requesters)
        def _():
            gather(0, t + 1, 0)

        pack(1, t, 1)
        pltpu.make_async_copy(second.at[t], second_hbm.at[t], sems.at[parts + 1]).start()

    pltpu.make_async_copy(second, second_hbm, sems.at[parts + 1]).wait()


def serve_rows(got, tables, requesters, per_chunk):
    hashes, rows, width = tables.shape
    tiles = width // 128
    shape = (requesters, per_chunk, width)
    hbm = pl.BlockSpec(memory_space=pltpu.HBM)
    free = pl.BlockSpec(memory_space=pl.ANY)
    return pl.pallas_call(
        serve_kernel,
        out_shape=[jax.ShapeDtypeStruct(shape, BF)] * CHUNKS,
        in_specs=[free, hbm],
        out_specs=[pl.BlockSpec(memory_space=pltpu.VMEM), hbm],
        scratch_shapes=[
            pltpu.SMEM((got.shape[0], 128), jnp.int32),
            pltpu.VMEM(tables.shape, BF),
            pltpu.VMEM((hashes * rows * tiles, 128), F32),
            pltpu.VMEM((2, per_chunk * tiles, 128), F32),
            pltpu.VMEM(shape, BF),
            pltpu.SemaphoreType.DMA((2 * hashes + 2,)),
        ],
        compiler_params=pltpu.CompilerParams(vmem_limit_bytes=SERVE_VMEM),
        name="serve_rows",
    )(got, tables)


def sigmoid(z):
    return 0.5 + 0.5 * jnp.tanh(0.5 * z)


def layer_kernel(chunk, *refs):
    len_hbm, got_hbm, fetched, cot_hbm, w_in_hbm, w_out_hbm = refs[:6]
    enc_hbm, grad_hbm, *refs = refs[7:] if chunk else refs[6:]
    lengths, got, cot, enc, grads, w_in, w_out, x_s, n_s, gate_s, *refs = refs
    dsilu_s, qkv_s, mixed_s, s_s, w_s, dw_s, dz_s, mask_s, sems = refs
    users, length, width = cot.shape
    tokens = users * length
    head = width // HEADS
    owners, per_chunk, _ = fetched.shape
    halves = 1
    half_users = users // halves
    half_tokens = tokens // halves
    half_rows = per_chunk // halves
    half_slots = owners * half_rows
    pair = 2 * length
    mine = lax.axis_index("table")
    our_users = pl.ds(chunk * users, users)

    def fetch(i, src, dst):
        copy = pltpu.make_async_copy(src, dst, sems.at[i])
        copy.start()
        return copy

    get_len = fetch(0, len_hbm, lengths)
    get_slots = [
        fetch(1 + j, got_hbm.at[pl.ds((chunk * users + j) * owners + mine, 1)], got.at[pl.ds(j, 1)])
        for j in range(users)
    ]
    sem_at = 1 + users
    get_w = {
        c: fetch(
            sem_at + c, w_in_hbm.at[0, :, pl.ds(c * width, width)], w_in.at[:, pl.ds(c * width, width)]
        )
        for c in PARTS_ORDER
    }
    sem_at += 4
    get_w_out = fetch(sem_at, w_out_hbm.at[0], w_out)
    get_cot = fetch(sem_at + 1, cot_hbm.at[our_users], cot)
    sem_at += 2

    get_len.wait()
    for copy in get_slots:
        copy.wait()
    slot_rows, slot_cols = [], []
    for i in range(halves):
        rows_of = []
        for h in range(3):
            packed = jnp.concatenate(
                [
                    got[i * half_users + j, :, 128 + h * length : 128 + (h + 1) * length]
                    for j in range(half_users)
                ],
                axis=1,
            )
            rows_of.append(
                lax.shift_right_logical(packed, 4) * half_rows
                + lax.div(iota((1, half_tokens), 1), length) * PER
                + (packed & 15)
            )
        stacked = jnp.concatenate(rows_of + [jnp.zeros((5, half_tokens), jnp.int32)], axis=0)
        slot_rows.append(rows_of)
        slot_cols.append(stacked.astype(F32).T.astype(jnp.int32))
    picks = []
    for i in range(halves):
        lane = iota((half_tokens, half_slots), 1)
        pick = (lane == slot_cols[i][:, 0:1]) | (lane == slot_cols[i][:, 1:2])
        pick = pick | (lane == slot_cols[i][:, 2:3])
        picks.append(jnp.where(pick, 1.0, 0.0).astype(BF))

    token_user = lax.div(iota((tokens, 1), 0), length)
    token_pos = iota((tokens, 1), 0) - token_user * length
    token_len = jnp.zeros((tokens, 1), jnp.int32)
    for u in range(users):
        token_len = jnp.where(token_user == u, lengths[chunk * users + u], token_len)
    live = jnp.where(token_pos < token_len, 1.0, 0.0).astype(F32)
    key = iota((tokens, pair), 1)
    query = iota((tokens, pair), 0)
    same = lax.div(key, length) == lax.rem(lax.div(query, length), 2)
    causal = lax.rem(key, length) <= lax.rem(query, length)
    mask_s[...] = jnp.where(same & causal, 1.0, 0.0) * live

    for i in range(halves):
        rows = slice(i * half_tokens, (i + 1) * half_tokens)
        block = fetched[:, i * half_rows : (i + 1) * half_rows, :].reshape(half_slots, width)
        x_s[rows] = dot(picks[i], block).astype(BF).astype(F32)
    x = x_s[...]
    mean = jnp.mean(x, axis=1, keepdims=True)
    centered = x - mean
    rstd = lax.rsqrt(jnp.mean(centered * centered, axis=1, keepdims=True) + EPS)
    n_s[...] = (centered * rstd).astype(BF)

    step = STEP
    for c in PARTS_ORDER:
        get_w[c].wait()

        @pl.loop(0, width // step)
        def _(i, c=c):
            cols = pl.ds(pl.multiple_of(i * step, step), step)
            z = dot(n_s[...], w_in[:, pl.ds(pl.multiple_of(c * width + i * step, step), step)])
            sig = sigmoid(z)
            out = z * sig
            dsilu_s[c, :, cols] = sig + out * (1.0 - sig)
            if c == 0:
                gate_s[:, cols] = out
            else:
                qkv_s[c - 1, :, cols] = out.astype(BF)

    scale = head ** (-0.5)
    blocks = [
        (slice(p * pair, (p + 1) * pair), slice(h * head, (h + 1) * head))
        for h in range(HEADS)
        for p in range(tokens // pair)
    ]
    for at in blocks:
        s_s[at] = dot(qkv_s[(1, *at)], qkv_s[(2, *at)], NT)
    mask = mask_s[...]
    for h in range(HEADS):
        cols = slice(h * head, (h + 1) * head)
        s = s_s[:, cols] * scale
        sig = sigmoid(s)
        out = s * sig
        w_s[:, cols] = (out * mask).astype(BF)
        dw_s[:, cols] = (sig + out * (1.0 - sig)) * (mask * scale)
    for at in blocks:
        mixed_s[at] = dot(w_s[at], qkv_s[(0, *at)])

    mixed = mixed_s[...]
    mean2 = jnp.mean(mixed, axis=1, keepdims=True)
    centered2 = mixed - mean2
    rstd2 = lax.rsqrt(jnp.mean(centered2 * centered2, axis=1, keepdims=True) + EPS)
    hat = centered2 * rstd2
    gate = gate_s[...]
    gated = (hat * gate).astype(BF)
    get_w_out.wait()
    out = (x_s[...] + dot(gated, w_out[...])) * live
    enc[...] = out.astype(BF).reshape(users, length, width)
    send_enc = fetch(sem_at, enc, enc_hbm.at[our_users])
    sem_at += 1

    get_cot.wait()
    g = cot[...].reshape(tokens, width).astype(F32) * live
    dgated = dot(g.astype(BF), w_out[...], NT).astype(BF).astype(F32)
    dz_s[0] = (dgated * hat * dsilu_s[0]).astype(BF)
    dhat = dgated * gate
    dmixed = rstd2 * (
        dhat
        - jnp.mean(dhat, axis=1, keepdims=True)
        - hat * jnp.mean(dhat * hat, axis=1, keepdims=True)
    )
    n_s[...] = dmixed.astype(BF)
    for at in blocks:
        s_s[at] = dot(n_s[at], qkv_s[(0, *at)], NT)
    for at in blocks:
        dv = dot(w_s[at], n_s[at], TN).astype(BF).astype(F32)
        dz_s[(1, *at)] = (dv * dsilu_s[(1, *at)]).astype(BF)
    for h in range(HEADS):
        cols = slice(h * head, (h + 1) * head)
        w_s[:, cols] = (s_s[:, cols].astype(BF).astype(F32) * dw_s[:, cols]).astype(BF)
    for at in blocks:
        dq = dot(w_s[at], qkv_s[(2, *at)]).astype(BF).astype(F32)
        dz_s[(2, *at)] = (dq * dsilu_s[(2, *at)]).astype(BF)
    for at in blocks:
        dk = dot(w_s[at], qkv_s[(1, *at)], TN).astype(BF).astype(F32)
        dz_s[(3, *at)] = (dk * dsilu_s[(3, *at)]).astype(BF)

    @pl.loop(0, width // step)
    def _(i):
        cols = pl.ds(pl.multiple_of(i * step, step), step)
        dn = dot(dz_s[0], w_in[cols, :width], NT)
        for c in range(1, 4):
            dn = dn + dot(dz_s[c], w_in[cols, c * width : (c + 1) * width], NT)
        mixed_s[:, cols] = dn

    dn = mixed_s[...].astype(BF).astype(F32)
    xhat = (x_s[...] - mean) * rstd
    dx = rstd * (
        dn
        - jnp.mean(dn, axis=1, keepdims=True)
        - xhat * jnp.mean(dn * xhat, axis=1, keepdims=True)
    )
    n_s[...] = (dx + g).astype(BF)
    puts = []
    for i in range(halves):
        sub = iota((half_slots, half_tokens), 0)
        put = (sub == slot_rows[i][0]) | (sub == slot_rows[i][1]) | (sub == slot_rows[i][2])
        puts.append(jnp.where(put, 1.0, 0.0).astype(BF))
    ranks = grads.shape[0]
    copies = [send_enc]
    for b in range(0, ranks, 2):
        cols = slice(b * 128, (b + 2) * 128)
        for i in range(halves):
            rows = slice(i * half_tokens, (i + 1) * half_tokens)
            two = dot(puts[i], n_s[rows, cols]).astype(BF)
            for r in range(2):
                grads[b + r, :, i * half_rows : (i + 1) * half_rows, :] = two[
                    :, r * 128 : (r + 1) * 128
                ].reshape(owners, half_rows, 128)
        copies.append(fetch(sem_at, grads.at[pl.ds(b, 2)], grad_hbm.at[pl.ds(b, 2)]))
        sem_at += 1
    for copy in copies:
        copy.wait()


def layer(chunk, lengths, got, fetched, cot, w_in, w_out, batch_ranks, prev):
    owners, per_chunk, width = fetched.shape
    all_users, length, _ = cot.shape
    users = all_users // CHUNKS
    tokens = users * length
    ours = (users, length, width)
    grad_shape = (batch_ranks, owners, per_chunk, width // batch_ranks)
    hbm = pl.BlockSpec(memory_space=pltpu.HBM)
    free = pl.BlockSpec(memory_space=pl.ANY)
    vmem = pl.BlockSpec(memory_space=pltpu.VMEM)
    args = (lengths, got, fetched, cot, w_in, w_out) + ((prev,) if chunk else ())
    return pl.pallas_call(
        functools.partial(layer_kernel, chunk),
        out_shape=[
            jax.ShapeDtypeStruct(cot.shape, BF),
            jax.ShapeDtypeStruct(grad_shape, BF),
        ],
        in_specs=[hbm, free, vmem, hbm, hbm, hbm, hbm][: len(args)],
        out_specs=[hbm, hbm],
        input_output_aliases={6: 0} if chunk else {},
        scratch_shapes=[
            pltpu.SMEM((all_users,), jnp.int32),
            pltpu.VMEM((users, 1, got.shape[2]), jnp.int32),
            pltpu.VMEM(ours, BF),
            pltpu.VMEM(ours, BF),
            pltpu.VMEM(grad_shape, BF),
            pltpu.VMEM((width, 4 * width), BF),
            pltpu.VMEM((width, width), BF),
            pltpu.VMEM((tokens, width), F32),
            pltpu.VMEM((tokens, width), BF),
            pltpu.VMEM((tokens, width), F32),
            pltpu.VMEM((4, tokens, width), F32),
            pltpu.VMEM((3, tokens, width), BF),
            pltpu.VMEM((tokens, width), F32),
            pltpu.VMEM((tokens, width), F32),
            pltpu.VMEM((tokens, width), BF),
            pltpu.VMEM((tokens, width), F32),
            pltpu.VMEM((4, tokens, width), BF),
            pltpu.VMEM((tokens, 2 * length), F32),
            pltpu.SemaphoreType.DMA((10 + users + batch_ranks // 2,)),
        ],
        compiler_params=pltpu.CompilerParams(vmem_limit_bytes=LAYER_VMEM),
        cost_estimate=COST,
        name="layer",
    )(*args)


def arrange(chunk, got, codes, per_sender):
    group = codes.shape[1] // per_sender
    users = per_sender // PER
    lane = iota((OWNERS, 128), 1)
    for b in range(got.shape[0] // OWNERS):
        line = jnp.zeros((OWNERS, 128), jnp.int32)
        for j in range(users):
            home = (chunk * users + j) * OWNERS
            moved = pltpu.roll(got[home : home + OWNERS, 0, :], ((j - b) * PER) % 128, 1)
            line = jnp.where((lane >= j * PER) & (lane < (j + 1) * PER), moved, line)
        for t in range(OWNERS):
            sender = b * OWNERS + t
            first = (sender % group) * per_sender
            codes[sender // group : sender // group + 1, first : first + per_sender] = line[
                t : t + 1, :per_sender
            ]


def collect_kernel(chunk, given, rows, *refs):
    if chunk:
        prev_hbm, out_hbm, codes, wide, hits, out, prev, sems = refs
    else:
        out_hbm, next_hbm, got, codes, later, wide, hits, out, sems = refs
    senders, per_sender, cols = rows.shape
    groups, depth = codes.shape
    group = senders // groups
    parts = wide.shape[1] // cols
    height = out.shape[0] // parts
    if chunk:
        get_codes = pltpu.make_async_copy(given, codes, sems.at[0])
        get_prev = pltpu.make_async_copy(prev_hbm, prev, sems.at[1])
        get_codes.start()
        get_prev.start()
        get_codes.wait()
    else:
        get_ids = pltpu.make_async_copy(given.at[:, :, pl.ds(0, 128)], got, sems.at[0])
        get_ids.start()
        get_ids.wait()
        arrange(0, got, codes, per_sender)
    part_cols = lax.div(codes[...], height).astype(F32).T.astype(jnp.int32)
    for s in range(groups):
        inside = lax.rem(codes[s : s + 1, :], height)
        for q in range(height // 128):
            near = jnp.clip(inside - 128 * q, -1, 128).astype(F32).astype(BF)
            row = iota((128, depth), 0).astype(F32).astype(BF)
            hits[q * 128 : (q + 1) * 128, s * depth : (s + 1) * depth] = jnp.where(
                row == near, jnp.ones((), BF), jnp.zeros((), BF)
            )
        block = rows[s * group : (s + 1) * group].reshape(depth, cols)
        for p in range(parts):
            here = part_cols[:, s : s + 1] == p
            wide[s * depth : (s + 1) * depth, p * cols : (p + 1) * cols] = jnp.where(
                here, block, jnp.zeros_like(block)
            )
    acc = dot(hits[...], wide[...])
    if chunk:
        get_prev.wait()
    puts = []
    for p in range(parts):
        at = slice(p * height, (p + 1) * height)
        part = acc[:, p * cols : (p + 1) * cols]
        out[at, :] = part + prev[at, :] if chunk else part
        puts.append(pltpu.make_async_copy(out.at[at], out_hbm.at[at], sems.at[2 + p]))
        puts[-1].start()
    if not chunk:
        arrange(1, got, later, per_sender)
        puts.append(pltpu.make_async_copy(later, next_hbm, sems.at[1]))
        puts[-1].start()
    for put in puts:
        put.wait()


def collect(chunk, given, rows, prev, total):
    senders, per_sender, cols = rows.shape
    hbm = pl.BlockSpec(memory_space=pltpu.HBM)
    free = pl.BlockSpec(memory_space=pl.ANY)
    vmem = pl.BlockSpec(memory_space=pltpu.VMEM)
    code_shape = (senders // GROUP, GROUP * per_sender)
    result = jax.ShapeDtypeStruct((total, cols), F32)
    ordered = pltpu.VMEM(code_shape, jnp.int32)
    before = [] if chunk else [pltpu.VMEM((given.shape[0], 1, 128), jnp.int32)]
    return pl.pallas_call(
        functools.partial(collect_kernel, chunk),
        out_shape=result if chunk else [result, jax.ShapeDtypeStruct(code_shape, jnp.int32)],
        in_specs=[free, vmem, hbm] if chunk else [free, vmem],
        out_specs=hbm if chunk else [hbm, hbm],
        scratch_shapes=before
        + [ordered] * (1 if chunk else 2)
        + [
            pltpu.VMEM((senders * per_sender, PARTS * cols), BF),
            pltpu.VMEM((total // PARTS, senders * per_sender), BF),
            pltpu.VMEM((total, cols), F32),
        ]
        + ([pltpu.VMEM((total, cols), F32)] if chunk else [])
        + [pltpu.SemaphoreType.DMA((2 + PARTS,))],
        compiler_params=pltpu.CompilerParams(vmem_limit_bytes=COLLECT_VMEM),
        cost_estimate=COST,
        name="collect",
    )(*((given, rows, prev) if chunk else (given, rows)))


def body(item_rows, send_order, user_lengths, tables, w_in, w_out, out_grad):
    batch_ranks = lax.axis_size("batch")
    table_ranks = lax.axis_size("table")
    users, length, hashes = item_rows.shape
    rows_local = tables.shape[1]
    both = ("batch", "table")
    per_chunk = users // CHUNKS * PER

    leaving = leaving_ids(send_order, item_rows.transpose(2, 0, 1), table_ranks)
    got = lax.all_to_all(leaving, both, 0, 0, tiled=True)
    served = serve_rows(got, tables, table_ranks, per_chunk)
    encoded, returned = None, []
    for c in range(CHUNKS):
        fetched = lax.all_to_all(served[c], "table", 0, 0, tiled=True)
        encoded, grads = layer(
            c, user_lengths, got, fetched, out_grad, w_in, w_out, batch_ranks, encoded
        )
        grads = grads.reshape(batch_ranks * table_ranks, per_chunk, -1)
        returned.append(lax.all_to_all(grads, both, 0, 0, tiled=True))
    total, codes = collect(0, got, returned[0], None, hashes * rows_local)
    total = collect(1, codes, returned[1], total, hashes * rows_local)
    return encoded, total.reshape(hashes, rows_local, -1)


def solution(mesh):
    in_specs = (
        P(("batch", "table"), None, None),
        P(("batch", "table")),
        P(("batch", "table")),
        P(None, "table", None),
        P(),
        P(),
        P(("batch", "table"), None, None),
    )
    out_specs = (P(("batch", "table"), None, None), P(None, "table", "batch"))
    return jax.shard_map(body, mesh=mesh, in_specs=in_specs, out_specs=out_specs, check_vma=False)
```
